32 devices in a mesh: samp: 4 (over y, x), feat: 8 (over z, core).
Axes of the slice: x: 2, y: 2, z: 4, core: 2. Of those that a mesh axis runs over, the one named last changes fastest.
Arguments:
- data: float32 [4096, 16384], P('samp', 'feat'), may hold values from -0.07216878 to 0.07216878, as said below
- targets: float32 [4096, 128], P(('samp', 'feat')), may hold values from -36 to 36
- coef: float32 [16384, 128], P('feat'), may hold values from -6 to 6
- coef_dual: float32 [16384, 128], P('feat'), may hold values from -3 to 3
- tile_coef_dual: float32 [4, 16384, 128], P('samp', 'feat'), may hold values from -3 to 3
- share: float32 [4096, 128], P(('samp', 'feat')), may hold values from -36 to 36
- share_dual: float32 [4096, 128], P('samp'), may hold values from -6 to 6
- tile_share: float32 [8, 4096, 128], P('feat', 'samp'), may hold values from -6 to 6
Outputs:
- coef_out: float32 [16384, 128], P('feat')
- coef_dual_out: float32 [16384, 128], P('feat')
- tile_coef_dual_out: float32 [4, 16384, 128], P('samp', 'feat')
- share_out: float32 [4096, 128], P(('samp', 'feat'))
- share_dual_out: float32 [4096, 128], P('samp')
- tile_share_out: float32 [8, 4096, 128], P('feat', 'samp')
The draws below stay inside these ranges and needn't reach their ends.
Inputs may be any that keep to these rules, and one draw needn't show every extreme that they name: `data`: independent entries of mean zero and variance 1 / 3072.
All inputs are finite; a program needn't handle non-finite values.
Results may differ from the reference program's by a relative error of at most 0.0001.
Values sent between devices are 32-bit elements; how exact they have to be, the bound alone decides.
No kernel may reach another device: no remote copies, remote signals or barrier semaphores. Data moves between devices by JAX's collectives and lax.ppermute only.
A program may use at most 64 MiB of HBM per device.

```python
import jax
import jax.numpy as jnp
from jax import lax

K = 128
FEATURES = 16384
S_DEV = 1024
ITERS = 2
CHEB = 5
F_DEV = 2048
SAMPLES = 4096
N_SAMP = 4
N_FEAT = 8


def draw_data(key, part):
    scale = 1.0 / jnp.sqrt(jnp.float32(S_DEV + F_DEV))
    values = jnp.clip(jax.random.normal(key, (SAMPLES, FEATURES), jnp.float32), -4.0, 4.0)
    return values * scale


def block_levels(rng, extent, pieces, smallest, top_value):
    gain, own = 1.0, jax.random.fold_in(rng, 6)
    for dim, blocks in pieces:
        steps = jnp.exp(jax.random.uniform(jax.random.fold_in(own, dim), (blocks,), jnp.float32, smallest / len(pieces), top_value / len(pieces)))
        gain = gain * jnp.repeat(steps, extent[dim] // blocks).reshape([-1 if axis == dim else 1 for axis in range(len(extent))])
    return gain


def normal_values(stream_key, extent, spread, reach, cuts=(), kind=jnp.bfloat16):
    array = jax.random.normal(stream_key, extent, jnp.float32) * spread
    if len(cuts) > 0:
        array = block_levels(stream_key, extent, cuts, -0.22, 0.18) * array
    return jnp.clip(array, min=-reach, max=reach).astype(kind)


def setup_inputs(seed: int = 0) -> dict:
    streams_of = jax.random.split(jax.random.key(seed), 9)
    return {
        "data": draw_data(jax.random.fold_in(streams_of[8], 71), 0),
        "targets": normal_values(streams_of[1], (SAMPLES, K), 6.0, 36.0, ((0, 32),), jnp.float32),
        "coef": normal_values(streams_of[2], (FEATURES, K), 1.0, 6.0, ((0, 8),), jnp.float32),
        "coef_dual": normal_values(streams_of[3], (FEATURES, K), 0.5, 3.0, ((0, 8),), jnp.float32),
        "tile_coef_dual": normal_values(streams_of[4], (N_SAMP, FEATURES, K), 0.5, 3.0, ((0, 4), (1, 8)), jnp.float32),
        "share": normal_values(streams_of[5], (SAMPLES, K), 6.0, 36.0, ((0, 32),), jnp.float32),
        "share_dual": normal_values(streams_of[6], (SAMPLES, K), 1.0, 6.0, ((0, 4),), jnp.float32),
        "tile_share": normal_values(streams_of[7], (N_FEAT, SAMPLES, K), 1.0, 6.0, ((0, 8), (1, 4)), jnp.float32),
    }


cheb_low = 1.0
cheb_high = 3.2
l1_weight = 0.2
huber_width = 4.0


def chebyshev(apply_fn, rhs, start):
    theta = (cheb_high + cheb_low) / 2.0
    delta = (cheb_high - cheb_low) / 2.0
    sigma = theta / delta
    iterate = start
    resid = rhs - apply_fn(iterate)
    search = resid / theta
    rho_old = 1.0 / sigma
    for step in range(CHEB):
        iterate = iterate + search
        if step + 1 < CHEB:
            resid = resid - apply_fn(search)
            rho_new = 1.0 / (2.0 * sigma - rho_old)
            search = rho_new * rho_old * search + (2.0 * rho_new / delta) * resid
            rho_old = rho_new
    return iterate


def reference(data, targets, coef, coef_dual, tile_coef_dual, share, share_dual, tile_share):
    high = lax.Precision.HIGHEST
    blocks = data.reshape(N_SAMP, S_DEV, N_FEAT, F_DEV)
    for sweep in range(ITERS):
        value = coef - coef_dual
        half_coef = value - jnp.clip(value, -l1_weight, l1_weight)
        resid_t = share - share_dual - targets
        half_share = targets + resid_t - jnp.clip(resid_t / 2.0, -huber_width, huber_width)
        shares_grouped = jnp.transpose(tile_share.reshape(N_FEAT, N_SAMP, S_DEV, K), (1, 0, 2, 3))
        duals_grouped = share_dual.reshape(N_SAMP, S_DEV, K)
        coef_now = coef

        def group(items):
            tiles, xt_group, ys_group, dual_group = items
            tiles = jnp.transpose(tiles, (1, 0, 2))
            start = coef_now.reshape(N_FEAT, F_DEV, K) - xt_group.reshape(N_FEAT, F_DEV, K)
            outs_in = ys_group + dual_group[None]

            def apply_fn(vector):
                inner = jnp.einsum("jsf,jfk->jsk", tiles, vector, precision=high)
                return vector + jnp.einsum("jsf,jsk->jfk", tiles, inner, precision=high)

            rhs = start + jnp.einsum("jsf,jsk->jfk", tiles, outs_in, precision=high)
            proj_x = chebyshev(apply_fn, rhs, start)
            proj_y = jnp.einsum("jsf,jfk->jsk", tiles, proj_x, precision=high)
            return proj_x, proj_y

        proj_coef, proj_share = lax.map(group, (blocks, tile_coef_dual, shares_grouped, duals_grouped))
        coef_new = (half_coef + jnp.sum(proj_coef, axis=0).reshape(FEATURES, K)) / (N_SAMP + 1)
        share_sum = jnp.sum(proj_share, axis=1).reshape(SAMPLES, K)
        excess = (half_share - share_sum) / (N_FEAT + 1)
        share = half_share - excess
        tile_share = jnp.transpose(proj_share, (1, 0, 2, 3)).reshape(N_FEAT, SAMPLES, K) + excess[None]
        share_dual = share_dual + excess
        coef_dual = coef_dual + half_coef - coef_new
        tile_coef_dual = tile_coef_dual + proj_coef.reshape(N_SAMP, FEATURES, K) - coef_new[None]
        coef = coef_new
    return (coef, coef_dual, tile_coef_dual, share, share_dual, tile_share)
```

```python
import functools

import jax
import jax.numpy as jnp
from jax import lax
from jax.experimental import pallas as pl
from jax.experimental.pallas import tpu as pltpu
from jax.sharding import PartitionSpec as P

CHEB = 5

cheb_low = 1.0
cheb_high = 3.2
l1_weight = 0.2
huber_width = 4.0

F32 = jnp.float32
BF16 = jnp.bfloat16
MIB = 1 << 20


def chebyshev_coefs():
    theta = (cheb_high + cheb_low) / 2.0
    delta = (cheb_high - cheb_low) / 2.0
    sigma = theta / delta
    rho = 1.0 / sigma
    pairs = []
    for _ in range(CHEB - 1):
        rho_new = 1.0 / (2.0 * sigma - rho)
        pairs.append((rho_new * rho, 2.0 * rho_new / delta))
        rho = rho_new
    return theta, pairs


def split(value):
    high = value.astype(BF16)
    return high, (value - high.astype(F32)).astype(BF16)


def dot_nn(a, b):
    return jnp.dot(a, b, preferred_element_type=F32)


def dot_nt(a, b):
    return lax.dot_general(a, b, (((1,), (1,)), ((), ())), preferred_element_type=F32)


def prox_coef(value):
    return value - jnp.clip(value, -l1_weight, l1_weight)


def prox_share(share, dual, targets):
    resid = share - dual - targets
    return targets + resid - jnp.clip(resid / 2.0, -huber_width, huber_width)


class Plan:
    def __init__(self, axis, size, order):
        self.axis, self.size, self.order = axis, size, order
        self.levels = len(order) - 1
        self.chunks = 1 << self.levels

    def key(self):
        index = lax.axis_index(self.axis)
        key = 0
        for level in range(self.levels):
            bit = lax.rem(lax.div(index, 1 << self.order[level]), 2)
            key = key + bit * (1 << (self.levels - 1 - level))
        return key

    def place(self, location, key):
        out = 0
        for bit in range(self.levels):
            own = lax.rem(lax.div(key, 1 << bit), 2)
            out = out + ((1 - own) if (location >> bit) & 1 else own) * (1 << bit)
        return out

    def permute(self, value, bit):
        return lax.ppermute(value, self.axis, [(i, i ^ (1 << bit)) for i in range(self.size)])


def butterfly(parts):
    state = [(plan, keep, send) for plan, keep, send in parts]
    rounds = max(plan.levels for plan, _, _ in parts)
    current = [None] * len(state)
    for level in range(rounds):
        for n, (plan, keep, send) in enumerate(state):
            if level >= plan.levels:
                continue
            if level > 0:
                half = current[n].shape[0] // 2
                keep, send = current[n][:half], current[n][half:]
            current[n] = keep + plan.permute(send, plan.order[level])
    for n, (plan, _, _) in enumerate(state):
        current[n] = current[n] + plan.permute(current[n], plan.order[plan.levels])
    halves = [None] * len(state)
    for level in reversed(range(rounds)):
        for n, (plan, _, _) in enumerate(state):
            if level >= plan.levels:
                continue
            other = plan.permute(current[n], plan.order[level])
            halves[n] = (current[n], other)
            if level > 0:
                current[n] = jnp.concatenate([current[n], other], axis=0)
    return halves


class Sizes:
    def __init__(self, mesh_shape, data_shape, cols):
        self.n_samp, self.n_feat = mesh_shape["samp"], mesh_shape["feat"]
        self.rows, self.feats = data_shape
        self.cols = cols
        bits = (self.n_samp - 1).bit_length()
        order = list(range(bits))
        self.colors = [
            Plan("samp", self.n_samp, order[n % bits:] + order[: n % bits]) for n in range(2)
        ]
        self.feat_plan = Plan("feat", self.n_feat, list(range((self.n_feat - 1).bit_length())))
        self.color_rows = self.feats // 2
        self.coef_chunk = self.color_rows // self.colors[0].chunks
        self.share_chunk = self.rows // self.feat_plan.chunks
        self.own = self.rows // self.n_feat
        self.row_block = min(256, self.rows)
        self.feat_block = min(256, self.feats)


def coef_places(sz):
    out = []
    for color, plan in enumerate(sz.colors):
        key = plan.key()
        for location in range(plan.chunks):
            offset = color * sz.color_rows + plan.place(location, key) * sz.coef_chunk
            out.append((color, location, pl.multiple_of(offset, 8)))
    return out


def share_places(sz):
    key = sz.feat_plan.key()
    return [
        (location, pl.multiple_of(sz.feat_plan.place(location, key) * sz.share_chunk, 8))
        for location in range(sz.feat_plan.chunks)
    ]


def half_of(location, chunks, chunk_rows):
    half = chunks // 2
    return location // half, (location % half) * chunk_rows


def chebyshev_steps(sz, g_hi, g_lo, resid, search, search2, total, part):
    theta, pairs = chebyshev_coefs()
    cols, block = sz.cols, sz.row_block
    blocks = sz.rows // block
    search[...] = resid[...] * (1.0 / theta)
    total[...] = search[...]
    high, low = split(search[...])
    search2[:, :cols] = high
    search2[:, cols:] = low
    for step in range(CHEB):
        last = step + 1 == CHEB
        for r in range(blocks):
            rows = pl.ds(r * block, block)
            wide = dot_nn(g_hi[rows, :], search2[...])
            prod = wide[:, :cols] + wide[:, cols:] + dot_nn(g_lo[rows, :], search2[:, :cols])
            if step == 0:
                part[rows, :] = prod
            else:
                part[rows, :] += prod
            if not last:
                c_old, c_res = pairs[step]
                old = search[rows, :]
                res = resid[rows, :] - old - prod
                new = c_old * old + c_res * res
                resid[rows, :] = res
                search[rows, :] = new
                total[rows, :] += new
        if not last:
            high, low = split(search[...])
            search2[:, :cols] = high
            search2[:, cols:] = low


def spread_coef(sz, a_hi, a_lo, start, total, wide_t, proj):
    cols, block = sz.cols, sz.feat_block
    high, low = split(total[...].T)
    wide_t[:cols, :] = high
    wide_t[cols:, :] = low
    for f in range(sz.feats // block):
        columns = pl.ds(f * block, block)
        wide = dot_nn(wide_t[...], a_hi[:, columns])
        out = wide[:cols] + wide[cols:] + dot_nn(wide_t[:cols, :], a_lo[:, columns])
        proj[columns, :] = start[columns, :] + out.T


def emit_coef(sz, proj, keeps, sends):
    for color, location, offset in coef_places(sz):
        which, row = half_of(location, sz.colors[color].chunks, sz.coef_chunk)
        target = (keeps, sends)[which][color]
        target[pl.ds(row, sz.coef_chunk), :] = proj[pl.ds(offset, sz.coef_chunk), :]


def emit_share(sz, proj_share, half_share, scratch, keep, send):
    own = pl.ds(pl.multiple_of(lax.axis_index("feat") * sz.own, 8), sz.own)
    scratch[...] = proj_share[...]
    scratch[own, :] = scratch[own, :] - half_share
    for location, offset in share_places(sz):
        which, row = half_of(location, sz.feat_plan.chunks, sz.share_chunk)
        target = (keep, send)[which]
        target[pl.ds(row, sz.share_chunk), :] = scratch[pl.ds(offset, sz.share_chunk), :]


def first_kernel(sz, data, targets, coef, tile_dual, share, share_dual, tile_share,
                 a_hi_out, a_lo_out, g_hi_out, g_lo_out, keep0, keep1, send0, send1,
                 keep_s, send_s, dual_plus, out_sum, proj_share,
                 a32, a_hi, a_lo, g_hi, g_lo, start, start2, resid, search, search2, total, part,
                 wide_t, proj, in_sem, out_sem):
    cols, block = sz.cols, sz.row_block
    blocks = sz.rows // block
    loads = []
    for r in range(blocks):
        rows = pl.ds(r * block, block)
        copy = pltpu.make_async_copy(data.at[rows, :], a32.at[rows, :], in_sem.at[r])
        copy.start()
        loads.append(copy)
    start[...] = coef[...] - tile_dual[...]
    high, low = split(start[...])
    start2[:, :cols] = high
    start2[:, cols:] = low
    stores = []
    for r in range(blocks):
        rows = pl.ds(r * block, block)
        loads[r].wait()
        high, low = split(a32[rows, :])
        a_hi[rows, :] = high
        a_lo[rows, :] = low
        for n, (src, dst) in enumerate(((a_hi, a_hi_out), (a_lo, a_lo_out))):
            copy = pltpu.make_async_copy(src.at[rows, :], dst.at[rows, :], out_sem.at[2 * r + n])
            copy.start()
            stores.append(copy)
        wide = dot_nn(a_hi[rows, :], start2[...])
        prod = wide[:, :cols] + wide[:, cols:] + dot_nn(a_lo[rows, :], start2[:, :cols])
        proj_share[rows, :] = prod
        resid[rows, :] = tile_share[rows, :] + share_dual[rows, :] - prod
        for c in range(r + 1):
            others = pl.ds(c * block, block)
            gram = dot_nt(a_hi[rows, :], a_hi[others, :])
            cross = dot_nt(a_hi[rows, :], a_lo[others, :])
            if c == r:
                gram = 0.5 * gram + cross
                gram = gram + gram.T
            else:
                gram = gram + cross + dot_nt(a_lo[rows, :], a_hi[others, :])
            high, low = split(gram)
            g_hi[rows, others] = high
            g_lo[rows, others] = low
            if c != r:
                high, low = split(gram.T)
                g_hi[others, rows] = high
                g_lo[others, rows] = low
    for n, (src, dst) in enumerate(((g_hi, g_hi_out), (g_lo, g_lo_out))):
        copy = pltpu.make_async_copy(src, dst, out_sem.at[2 * blocks + n])
        copy.start()
        stores.append(copy)
    chebyshev_steps(sz, g_hi, g_lo, resid, search, search2, total, part)
    spread_coef(sz, a_hi, a_lo, start, total, wide_t, proj)
    emit_coef(sz, proj, (keep0, keep1), (send0, send1))
    dual_plus[...] = tile_dual[...] + proj[...]
    proj_share[...] += part[...]
    out_sum[...] = proj_share[...] + share_dual[...]
    own = pl.ds(pl.multiple_of(lax.axis_index("feat") * sz.own, 8), sz.own)
    half_share = prox_share(share[...], share_dual[own, :], targets[...])
    emit_share(sz, proj_share, half_share, resid, keep_s, send_s)
    for copy in stores:
        copy.wait()


def second_kernel(sz, a_hi_in, a_lo_in, g_hi_in, g_lo_in, sum00, sum01, sum10, sum11,
                  esum0, esum1, coef, coef_dual, dual_plus, out_sum, targets, share, share_dual,
                  keep0, keep1, send0, send1, keep_s, send_s,
                  half_out, coef_plus, tile_plus, half_share_out, share_dual_out, proj_share,
                  a_hi, a_lo, g_hi, g_lo, start, start2, resid, search, search2, total, part,
                  wide_t, proj, in_sem):
    cols, block = sz.cols, sz.row_block
    blocks = sz.rows // block
    loads = []
    for r in range(blocks):
        rows = pl.ds(r * block, block)
        for n, (src, dst) in enumerate(((a_hi_in, a_hi), (a_lo_in, a_lo))):
            copy = pltpu.make_async_copy(src.at[rows, :], dst.at[rows, :], in_sem.at[2 * r + n])
            copy.start()
            loads.append(copy)
    for n, (src, dst) in enumerate(((g_hi_in, g_hi), (g_lo_in, g_lo))):
        copy = pltpu.make_async_copy(src, dst, in_sem.at[2 * blocks + n])
        copy.start()
        loads.append(copy)
    sums = ((sum00, sum01), (sum10, sum11))
    for color, location, offset in coef_places(sz):
        rows = pl.ds(offset, sz.coef_chunk)
        which, row = half_of(location, sz.colors[color].chunks, sz.coef_chunk)
        total_coef = sums[color][which][pl.ds(row, sz.coef_chunk), :]
        dual = coef_dual[rows, :]
        half = prox_coef(coef[rows, :] - dual)
        new = (half + total_coef) / (sz.n_samp + 1)
        dual = dual + half - new
        half = prox_coef(new - dual)
        half_out[rows, :] = half
        coef_plus[rows, :] = dual + half
        tile = dual_plus[rows, :] - new
        tile_plus[rows, :] = tile
        first = new - tile
        start[rows, :] = first
        high, low = split(first)
        start2[rows, :cols] = high
        start2[rows, cols:] = low
    esums = (esum0, esum1)
    for location, offset in share_places(sz):
        rows = pl.ds(offset, sz.share_chunk)
        which, row = half_of(location, sz.feat_plan.chunks, sz.share_chunk)
        excess = esums[which][pl.ds(row, sz.share_chunk), :] * (-1.0 / (sz.n_feat + 1))
        search[rows, :] = excess
        share_dual_out[rows, :] = share_dual[rows, :] + excess
        resid[rows, :] = out_sum[rows, :] + 2.0 * excess
    own = pl.ds(pl.multiple_of(lax.axis_index("feat") * sz.own, 8), sz.own)
    share_now = prox_share(share[...], share_dual[own, :], targets[...]) - search[own, :]
    half_share = prox_share(share_now, share_dual_out[own, :], targets[...])
    half_share_out[...] = half_share
    for r in range(blocks):
        rows = pl.ds(r * block, block)
        loads[2 * r].wait()
        loads[2 * r + 1].wait()
        wide = dot_nn(a_hi[rows, :], start2[...])
        prod = wide[:, :cols] + wide[:, cols:] + dot_nn(a_lo[rows, :], start2[:, :cols])
        proj_share[rows, :] = prod
        resid[rows, :] = resid[rows, :] - prod
    loads[2 * blocks].wait()
    loads[2 * blocks + 1].wait()
    chebyshev_steps(sz, g_hi, g_lo, resid, search, search2, total, part)
    spread_coef(sz, a_hi, a_lo, start, total, wide_t, proj)
    emit_coef(sz, proj, (keep0, keep1), (send0, send1))
    tile_plus[...] += proj[...]
    proj_share[...] += part[...]
    emit_share(sz, proj_share, half_share, resid, keep_s, send_s)


def last_kernel(sz, sum00, sum01, sum10, sum11, esum0, esum1, half_coef, coef_plus, tile_plus,
                half_share, share_dual, proj_share,
                coef_out, coef_dual_out, tile_out, share_out, share_dual_out, tile_share_out):
    sums = ((sum00, sum01), (sum10, sum11))
    for color, location, offset in coef_places(sz):
        rows = pl.ds(offset, sz.coef_chunk)
        which, row = half_of(location, sz.colors[color].chunks, sz.coef_chunk)
        total_coef = sums[color][which][pl.ds(row, sz.coef_chunk), :]
        new = (half_coef[rows, :] + total_coef) / (sz.n_samp + 1)
        coef_out[rows, :] = new
        coef_dual_out[rows, :] = coef_plus[rows, :] - new
        tile_out[rows, :] = tile_plus[rows, :] - new
    esums = (esum0, esum1)
    for location, offset in share_places(sz):
        rows = pl.ds(offset, sz.share_chunk)
        which, row = half_of(location, sz.feat_plan.chunks, sz.share_chunk)
        excess = esums[which][pl.ds(row, sz.share_chunk), :] * (-1.0 / (sz.n_feat + 1))
        share_dual_out[rows, :] = share_dual[rows, :] + excess
        tile_share_out[rows, :] = proj_share[rows, :] + excess
    own = pl.ds(pl.multiple_of(lax.axis_index("feat") * sz.own, 8), sz.own)
    share_out[...] = half_share[...] - (share_dual_out[own, :] - share_dual[own, :])


def shards(mesh_shape, data, targets, coef, coef_dual, tile_coef_dual, share, share_dual, tile_share):
    cols = coef.shape[1]
    sz = Sizes(mesh_shape, data.shape, cols)
    rows, feats = data.shape
    blocks = rows // sz.row_block
    f32 = lambda *shape: jax.ShapeDtypeStruct(shape, F32)
    b16 = lambda *shape: jax.ShapeDtypeStruct(shape, BF16)
    vmem = pl.BlockSpec(memory_space=pltpu.VMEM)
    anyw = pl.BlockSpec(memory_space=pl.ANY)
    v32 = lambda *shape: pltpu.VMEM(shape, F32)
    v16 = lambda *shape: pltpu.VMEM(shape, BF16)
    params = pltpu.CompilerParams(vmem_limit_bytes=56 * MIB)
    flops = 2 * rows * feats * cols

    half_coef_rows = f32(sz.color_rows // 2, cols)
    half_share_rows = f32(rows // 2, cols)
    sends = [half_coef_rows] * 4 + [half_share_rows] * 2
    matrices = [v16(rows, feats)] * 2 + [v16(rows, rows)] * 2
    work = [
        v32(feats, cols), v16(feats, 2 * cols), v32(rows, cols), v32(rows, cols),
        v16(rows, 2 * cols), v32(rows, cols), v32(rows, cols), v16(2 * cols, rows),
        v32(feats, cols),
    ]
    tile_dual = tile_coef_dual[0]

    outs = pl.pallas_call(
        functools.partial(first_kernel, sz),
        out_shape=[b16(rows, feats)] * 2 + [b16(rows, rows)] * 2 + sends
        + [f32(feats, cols), f32(rows, cols), f32(rows, cols)],
        in_specs=[anyw] + [vmem] * 6,
        out_specs=[anyw] * 4 + [vmem] * 9,
        scratch_shapes=[v32(rows, feats)] + matrices + work
        + [pltpu.SemaphoreType.DMA((blocks,)), pltpu.SemaphoreType.DMA((2 * blocks + 2,))],
        compiler_params=params,
        cost_estimate=pl.CostEstimate(flops=30 * flops, bytes_accessed=32 * MIB, transcendentals=0),
        name="first",
    )(data, targets, coef, tile_dual, share, share_dual, tile_share[0])
    mats, (keep0, keep1, send0, send1, keep_s, send_s), (dual_plus, out_sum, _) = (
        outs[:4], outs[4:10], outs[10:])

    def sums(keep0, keep1, send0, send1, keep_s, send_s):
        return butterfly([
            (sz.colors[0], keep0, send0), (sz.colors[1], keep1, send1), (sz.feat_plan, keep_s, send_s)])

    (s00, s01), (s10, s11), (e0, e1) = sums(keep0, keep1, send0, send1, keep_s, send_s)
    outs = pl.pallas_call(
        functools.partial(second_kernel, sz),
        out_shape=sends + [f32(feats, cols)] * 3
        + [f32(sz.own, cols), f32(rows, cols), f32(rows, cols)],
        in_specs=[anyw] * 4 + [vmem] * 13,
        out_specs=[vmem] * 12,
        scratch_shapes=matrices + work + [pltpu.SemaphoreType.DMA((2 * blocks + 2,))],
        compiler_params=params,
        cost_estimate=pl.CostEstimate(flops=14 * flops, bytes_accessed=20 * MIB, transcendentals=0),
        name="second",
    )(*mats, s00, s01, s10, s11, e0, e1, coef, coef_dual, dual_plus, out_sum, targets, share, share_dual)
    half_coef, coef_plus, tile_plus, half_share, dual_now, proj_share = outs[6:]
    (s00, s01), (s10, s11), (e0, e1) = sums(*outs[:6])
    coef_out, coef_dual_out, tile_out, share_out, share_dual_out, tile_share_out = pl.pallas_call(
        functools.partial(last_kernel, sz),
        out_shape=[f32(feats, cols)] * 3 + [f32(sz.own, cols), f32(rows, cols), f32(rows, cols)],
        in_specs=[vmem] * 12,
        out_specs=[vmem] * 6,
        compiler_params=params,
        cost_estimate=pl.CostEstimate(flops=feats * cols * 8, bytes_accessed=10 * MIB, transcendentals=0),
        name="last",
    )(s00, s01, s10, s11, e0, e1, half_coef, coef_plus, tile_plus, half_share, dual_now, proj_share)
    return (coef_out, coef_dual_out, tile_out[None], share_out, share_dual_out, tile_share_out[None])


def solution(mesh):
    mesh_shape = dict(mesh.shape)
    return jax.shard_map(
        functools.partial(shards, mesh_shape),
        mesh=mesh,
        in_specs=(
            P("samp", "feat"),
            P(("samp", "feat"), None),
            P("feat", None),
            P("feat", None),
            P("samp", "feat", None),
            P(("samp", "feat"), None),
            P("samp", None),
            P("feat", "samp", None),
        ),
        out_specs=(
            P("feat", None),
            P("feat", None),
            P("samp", "feat", None),
            P(("samp", "feat"), None),
            P("samp", None),
            P("feat", "samp", None),
        ),
        check_vma=False,
    )
```

```python
import functools

import jax
import jax.numpy as jnp
from jax import lax
from jax.experimental import pallas as pl
from jax.experimental.pallas import tpu as pltpu
from jax.sharding import PartitionSpec as P

CHEB = 5

cheb_low = 1.0
cheb_high = 3.2
l1_weight = 0.2
huber_width = 4.0

F32 = jnp.float32
BF16 = jnp.bfloat16
MIB = 1 << 20
LIMIT = 16


def chebyshev_coefs():
    theta = (cheb_high + cheb_low) / 2.0
    delta = (cheb_high - cheb_low) / 2.0
    sigma = theta / delta
    rho = 1.0 / sigma
    pairs = []
    for _ in range(CHEB - 1):
        rho_new = 1.0 / (2.0 * sigma - rho)
        pairs.append((rho_new * rho, 2.0 * rho_new / delta))
        rho = rho_new
    return theta, pairs


def split(value):
    high = value.astype(BF16)
    return high, (value - high.astype(F32)).astype(BF16)


def dot_nn(a, b):
    return jnp.dot(a, b, preferred_element_type=F32)


def dot_nt(a, b):
    return lax.dot_general(a, b, (((1,), (1,)), ((), ())), preferred_element_type=F32)


def prox_coef(value):
    return value - jnp.clip(value, -l1_weight, l1_weight)


def prox_share(share, dual, targets):
    resid = share - dual - targets
    return targets + resid - jnp.clip(resid / 2.0, -huber_width, huber_width)


class Plan:
    def __init__(self, axis, size, order):
        self.axis, self.size, self.order = axis, size, order
        self.levels = len(order) - 1
        self.chunks = 1 << self.levels

    def key(self):
        index = lax.axis_index(self.axis)
        key = 0
        for level in range(self.levels):
            bit = lax.rem(lax.div(index, 1 << self.order[level]), 2)
            key = key + bit * (1 << (self.levels - 1 - level))
        return key

    def place(self, location, key):
        out = 0
        for bit in range(self.levels):
            own = lax.rem(lax.div(key, 1 << bit), 2)
            out = out + ((1 - own) if (location >> bit) & 1 else own) * (1 << bit)
        return out

    def permute(self, value, bit):
        return lax.ppermute(value, self.axis, [(i, i ^ (1 << bit)) for i in range(self.size)])


def butterfly(parts):
    state = [(plan, keep, send) for plan, keep, send in parts]
    rounds = max(plan.levels for plan, _, _ in parts)
    current = [None] * len(state)
    for level in range(rounds):
        for n, (plan, keep, send) in enumerate(state):
            if level >= plan.levels:
                continue
            if level > 0:
                half = current[n].shape[0] // 2
                keep, send = current[n][:half], current[n][half:]
            current[n] = keep + plan.permute(send, plan.order[level])
    for n, (plan, _, _) in enumerate(state):
        current[n] = current[n] + plan.permute(current[n], plan.order[plan.levels])
    halves = [None] * len(state)
    for level in reversed(range(rounds)):
        for n, (plan, _, _) in enumerate(state):
            if level >= plan.levels:
                continue
            other = plan.permute(current[n], plan.order[level])
            halves[n] = (current[n], other)
            if level > 0:
                current[n] = jnp.concatenate([current[n], other], axis=0)
    return halves


class Sizes:
    def __init__(self, mesh_shape, data_shape, cols):
        self.n_samp, self.n_feat = mesh_shape["samp"], mesh_shape["feat"]
        self.rows, self.feats = data_shape
        self.cols = cols
        bits = (self.n_samp - 1).bit_length()
        order = list(range(bits))
        self.colors = [
            Plan("samp", self.n_samp, order[n % bits:] + order[: n % bits]) for n in range(2)
        ]
        self.feat_plan = Plan("feat", self.n_feat, list(range((self.n_feat - 1).bit_length())))
        self.color_rows = self.feats // 2
        self.coef_chunk = self.color_rows // self.colors[0].chunks
        self.share_chunk = self.rows // self.feat_plan.chunks
        self.own = self.rows // self.n_feat
        self.row_block = min(256, self.rows)
        self.feat_block = min(256, self.feats)


def coef_places(sz):
    out = []
    for color, plan in enumerate(sz.colors):
        key = plan.key()
        for location in range(plan.chunks):
            offset = color * sz.color_rows + plan.place(location, key) * sz.coef_chunk
            out.append((color, location, pl.multiple_of(offset, 8)))
    return out


def share_places(sz):
    key = sz.feat_plan.key()
    return [
        (location, pl.multiple_of(sz.feat_plan.place(location, key) * sz.share_chunk, 8))
        for location in range(sz.feat_plan.chunks)
    ]


def half_of(location, chunks, chunk_rows):
    half = chunks // 2
    return location // half, (location % half) * chunk_rows


def put_split(target, rows, cols, value):
    high, low = split(value)
    target[rows, :cols] = high
    target[rows, cols:] = low


def put_wide(wide_t, cols, value):
    high, low = split(value.T)
    wide_t[:cols, :] = high
    wide_t[cols:, :] = low


def triple(a_hi, a_lo, rows, value2, cols):
    wide = dot_nn(a_hi[rows, :], value2[...])
    return wide[:, :cols] + wide[:, cols:] + dot_nn(a_lo[rows, :], value2[:, :cols])


def chebyshev_steps(sz, g_hi, g_lo, resid, search, search2, total, part):
    theta, pairs = chebyshev_coefs()
    cols, block = sz.cols, sz.row_block
    blocks = [pl.ds(r * block, block) for r in range(sz.rows // block)]
    for rows in blocks:
        first = resid[rows, :] * (1.0 / theta)
        search[rows, :] = first
        total[rows, :] = first
        put_split(search2.at[0], rows, cols, first)
    for step in range(CHEB):
        last = step + 1 == CHEB
        now, later = search2.at[step % 2], search2.at[(step + 1) % 2]
        for rows in blocks:
            prod = triple(g_hi, g_lo, rows, now, cols)
            if step == 0:
                part[rows, :] = prod
            else:
                part[rows, :] += prod
            if not last:
                c_old, c_res = pairs[step]
                old = search[rows, :]
                res = resid[rows, :] - old - prod
                new = c_old * old + c_res * res
                resid[rows, :] = res
                search[rows, :] = new
                total[rows, :] += new
                put_split(later, rows, cols, new)


def spread_kernel(sz, wide_t, a_hi, a_lo, start, dual, keep0, keep1, send0, send1, plus, proj):
    cols, block = sz.cols, sz.feat_block
    for f in range(sz.feats // block):
        columns = pl.ds(f * block, block)
        wide = dot_nn(wide_t[...], a_hi[:, columns])
        out = wide[:cols] + wide[cols:] + dot_nn(wide_t[:cols, :], a_lo[:, columns])
        value = start[columns, :] + out.T
        proj[columns, :] = value
        plus[columns, :] = dual[columns, :] + value
    emit_coef(sz, proj, (keep0, keep1), (send0, send1))


def emit_coef(sz, proj, keeps, sends):
    for color, location, offset in coef_places(sz):
        which, row = half_of(location, sz.colors[color].chunks, sz.coef_chunk)
        target = (keeps, sends)[which][color]
        target[pl.ds(row, sz.coef_chunk), :] = proj[pl.ds(offset, sz.coef_chunk), :]


def emit_share(sz, scratch, half_share, keep, send):
    own = pl.ds(pl.multiple_of(lax.axis_index("feat") * sz.own, 8), sz.own)
    scratch[own, :] = scratch[own, :] - half_share
    for location, offset in share_places(sz):
        which, row = half_of(location, sz.feat_plan.chunks, sz.share_chunk)
        target = (keep, send)[which]
        target[pl.ds(row, sz.share_chunk), :] = scratch[pl.ds(offset, sz.share_chunk), :]


def first_kernel(sz, data, coef, tile_dual, share, share_dual, targets, tile_share,
                 a_hi, a_lo, g_hi, g_lo, start, wide_t, keep_s, send_s, out_sum,
                 a32, start2, resid, search, search2, total, part, in_sem):
    cols, block = sz.cols, sz.row_block
    blocks = sz.rows // block
    loads = []
    for r in range(blocks):
        rows = pl.ds(r * block, block)
        copy = pltpu.make_async_copy(data.at[rows, :], a32.at[rows, :], in_sem.at[r])
        copy.start()
        loads.append(copy)
    first = coef[...] - tile_dual[...]
    start[...] = first
    put_split(start2, slice(None), cols, first)
    for r in range(blocks):
        rows = pl.ds(r * block, block)
        loads[r].wait()
        high, low = split(a32[rows, :])
        a_hi[rows, :] = high
        a_lo[rows, :] = low
        prod = triple(a_hi, a_lo, rows, start2, cols)
        out_sum[rows, :] = prod
        resid[rows, :] = tile_share[rows, :] + share_dual[rows, :] - prod
        for c in range(r + 1):
            others = pl.ds(c * block, block)
            gram = dot_nt(a_hi[rows, :], a_hi[others, :])
            cross = dot_nt(a_hi[rows, :], a_lo[others, :])
            if c == r:
                gram = 0.5 * gram + cross
                gram = gram + gram.T
            else:
                gram = gram + cross + dot_nt(a_lo[rows, :], a_hi[others, :])
            high, low = split(gram)
            g_hi[rows, others] = high
            g_lo[rows, others] = low
            if c != r:
                high, low = split(gram.T)
                g_hi[others, rows] = high
                g_lo[others, rows] = low
    chebyshev_steps(sz, g_hi, g_lo, resid, search, search2, total, part)
    put_wide(wide_t, cols, total[...])
    part[...] += out_sum[...]
    out_sum[...] = part[...] + share_dual[...]
    own = pl.ds(pl.multiple_of(lax.axis_index("feat") * sz.own, 8), sz.own)
    half_share = prox_share(share[...], share_dual[own, :], targets[...])
    emit_share(sz, part, half_share, keep_s, send_s)


def second_kernel(sz, a_hi, a_lo, g_hi, g_lo, sum00, sum01, sum10, sum11,
                  esum0, esum1, coef, coef_dual, dual_plus, out_sum, targets, share, share_dual,
                  start, tile_now, half_out, coef_plus, wide_t, keep_s, send_s,
                  half_share_out, share_dual_out, proj_share,
                  start2, resid, search, search2, total, part):
    cols, block = sz.cols, sz.row_block
    sums = ((sum00, sum01), (sum10, sum11))
    for color, location, offset in coef_places(sz):
        rows = pl.ds(offset, sz.coef_chunk)
        which, row = half_of(location, sz.colors[color].chunks, sz.coef_chunk)
        total_coef = sums[color][which][pl.ds(row, sz.coef_chunk), :]
        dual = coef_dual[rows, :]
        half = prox_coef(coef[rows, :] - dual)
        new = (half + total_coef) / (sz.n_samp + 1)
        dual = dual + half - new
        half = prox_coef(new - dual)
        half_out[rows, :] = half
        coef_plus[rows, :] = dual + half
        tile = dual_plus[rows, :] - new
        tile_now[rows, :] = tile
        first = new - tile
        start[rows, :] = first
        put_split(start2, rows, cols, first)
    esums = (esum0, esum1)
    for location, offset in share_places(sz):
        rows = pl.ds(offset, sz.share_chunk)
        which, row = half_of(location, sz.feat_plan.chunks, sz.share_chunk)
        excess = esums[which][pl.ds(row, sz.share_chunk), :] * (-1.0 / (sz.n_feat + 1))
        search[rows, :] = excess
        share_dual_out[rows, :] = share_dual[rows, :] + excess
        resid[rows, :] = out_sum[rows, :] + 2.0 * excess
    own = pl.ds(pl.multiple_of(lax.axis_index("feat") * sz.own, 8), sz.own)
    share_now = prox_share(share[...], share_dual[own, :], targets[...]) - search[own, :]
    half_share = prox_share(share_now, share_dual_out[own, :], targets[...])
    half_share_out[...] = half_share
    for r in range(sz.rows // block):
        rows = pl.ds(r * block, block)
        prod = triple(a_hi, a_lo, rows, start2, cols)
        proj_share[rows, :] = prod
        resid[rows, :] = resid[rows, :] - prod
    chebyshev_steps(sz, g_hi, g_lo, resid, search, search2, total, part)
    put_wide(wide_t, cols, total[...])
    part[...] += proj_share[...]
    proj_share[...] = part[...]
    emit_share(sz, part, half_share, keep_s, send_s)


def last_kernel(sz, sum00, sum01, sum10, sum11, esum0, esum1, half_coef, coef_plus, tile_plus,
                half_share, share_dual, proj_share,
                coef_out, coef_dual_out, tile_out, share_out, share_dual_out, tile_share_out):
    sums = ((sum00, sum01), (sum10, sum11))
    for color, location, offset in coef_places(sz):
        rows = pl.ds(offset, sz.coef_chunk)
        which, row = half_of(location, sz.colors[color].chunks, sz.coef_chunk)
        total_coef = sums[color][which][pl.ds(row, sz.coef_chunk), :]
        new = (half_coef[rows, :] + total_coef) / (sz.n_samp + 1)
        coef_out[rows, :] = new
        coef_dual_out[rows, :] = coef_plus[rows, :] - new
        tile_out[rows, :] = tile_plus[rows, :] - new
    esums = (esum0, esum1)
    for location, offset in share_places(sz):
        rows = pl.ds(offset, sz.share_chunk)
        which, row = half_of(location, sz.feat_plan.chunks, sz.share_chunk)
        excess = esums[which][pl.ds(row, sz.share_chunk), :] * (-1.0 / (sz.n_feat + 1))
        share_dual_out[rows, :] = share_dual[rows, :] + excess
        tile_share_out[rows, :] = proj_share[rows, :] + excess
    own = pl.ds(pl.multiple_of(lax.axis_index("feat") * sz.own, 8), sz.own)
    share_out[...] = half_share[...] - (share_dual_out[own, :] - share_dual[own, :])


def shards(mesh_shape, data, targets, coef, coef_dual, tile_coef_dual, share, share_dual, tile_share):
    cols = coef.shape[1]
    sz = Sizes(mesh_shape, data.shape, cols)
    rows, feats = data.shape
    blocks = rows // sz.row_block
    f32 = lambda *shape: jax.ShapeDtypeStruct(shape, F32)
    v32 = lambda *shape: pltpu.VMEM(shape, F32)
    v16 = lambda *shape: pltpu.VMEM(shape, BF16)
    flops = 2 * rows * feats * cols

    def kernel(body, name, outs, scratch, work, limit, *operands, streamed=0):
        vmem = pl.BlockSpec(memory_space=pltpu.VMEM)
        hbm = pl.BlockSpec(memory_space=pltpu.HBM)
        return pl.pallas_call(
            functools.partial(body, sz),
            out_shape=outs,
            in_specs=[hbm] * streamed + [vmem] * (len(operands) - streamed),
            out_specs=[vmem] * len(outs),
            scratch_shapes=scratch,
            compiler_params=pltpu.CompilerParams(vmem_limit_bytes=limit * MIB),
            cost_estimate=pl.CostEstimate(flops=work, bytes_accessed=8 * MIB, transcendentals=0),
            name=name,
        )(*operands)

    coef_sends = [v32(sz.color_rows // 2, cols)] * 4
    share_sends = [v32(rows // 2, cols)] * 2
    matrices = [v16(rows, feats)] * 2 + [v16(rows, rows)] * 2
    vector = v32(rows, cols)
    wide_t = v16(2 * cols, rows)
    work = [v16(feats, 2 * cols), vector, vector, v16(2, rows, 2 * cols), vector, vector]
    tile_dual = tile_coef_dual[0]

    def spread(wide, a_hi, a_lo, start, dual):
        return kernel(
            spread_kernel, "spread", coef_sends + [v32(feats, cols)], [v32(feats, cols)], 3 * flops, LIMIT,
            wide, a_hi, a_lo, start, dual)

    def sums(keep0, keep1, send0, send1, keep_s, send_s):
        return butterfly([
            (sz.colors[0], keep0, send0), (sz.colors[1], keep1, send1), (sz.feat_plan, keep_s, send_s)])

    a_hi, a_lo, g_hi, g_lo, start, wide, keep_s, send_s, out_sum = kernel(
        first_kernel, "first", matrices + [v32(feats, cols), wide_t] + share_sends + [vector],
        [v32(rows, feats)] + work + [pltpu.SemaphoreType.DMA((blocks,))], 30 * flops, LIMIT,
        data, coef, tile_dual, share, share_dual, targets, tile_share[0], streamed=1)
    *parts, dual_plus = spread(wide, a_hi, a_lo, start, tile_dual)
    (s00, s01), (s10, s11), (e0, e1) = sums(*parts, keep_s, send_s)
    (start, tile_now, half_coef, coef_plus, wide, keep_s, send_s, half_share, dual_now,
     proj_share) = kernel(
        second_kernel, "second",
        [v32(feats, cols)] * 4 + [wide_t] + share_sends + [v32(sz.own, cols), vector, vector],
        work, 11 * flops, LIMIT,
        a_hi, a_lo, g_hi, g_lo, s00, s01, s10, s11, e0, e1, coef, coef_dual, dual_plus, out_sum,
        targets, share, share_dual)
    *parts, tile_plus = spread(wide, a_hi, a_lo, start, tile_now)
    (s00, s01), (s10, s11), (e0, e1) = sums(*parts, keep_s, send_s)
    coef_out, coef_dual_out, tile_out, share_out, share_dual_out, tile_share_out = kernel(
        last_kernel, "last",
        [f32(feats, cols)] * 3 + [f32(sz.own, cols), f32(rows, cols), f32(rows, cols)],
        [], flops // 100, LIMIT,
        s00, s01, s10, s11, e0, e1, half_coef, coef_plus, tile_plus, half_share, dual_now, proj_share)
    return (coef_out, coef_dual_out, tile_out[None], share_out, share_dual_out, tile_share_out[None])


def solution(mesh):
    mesh_shape = dict(mesh.shape)
    return jax.shard_map(
        functools.partial(shards, mesh_shape),
        mesh=mesh,
        in_specs=(
            P("samp", "feat"),
            P(("samp", "feat"), None),
            P("feat", None),
            P("feat", None),
            P("samp", "feat", None),
            P(("samp", "feat"), None),
            P("samp", None),
            P("feat", "samp", None),
        ),
        out_specs=(
            P("feat", None),
            P("feat", None),
            P("samp", "feat", None),
            P(("samp", "feat"), None),
            P("samp", None),
            P("feat", "samp", None),
        ),
        check_vma=False,
    )
```

```python
import functools

import jax
import jax.numpy as jnp
from jax import lax
from jax.experimental import pallas as pl
from jax.experimental.pallas import tpu as pltpu
from jax.sharding import PartitionSpec as P

CHEB = 5

cheb_low = 1.0
cheb_high = 3.2
l1_weight = 0.2
huber_width = 4.0

F32 = jnp.float32
BF16 = jnp.bfloat16
MIB = 1 << 20
LIMIT = 16
HALVES = 1


def chebyshev_coefs():
    theta = (cheb_high + cheb_low) / 2.0
    delta = (cheb_high - cheb_low) / 2.0
    sigma = theta / delta
    rho = 1.0 / sigma
    pairs = []
    for _ in range(CHEB - 1):
        rho_new = 1.0 / (2.0 * sigma - rho)
        pairs.append((rho_new * rho, 2.0 * rho_new / delta))
        rho = rho_new
    return theta, pairs


def split(value):
    high = value.astype(BF16)
    return high, (value - high.astype(F32)).astype(BF16)


def dot_nn(a, b):
    return jnp.dot(a, b, preferred_element_type=F32)


def dot_nt(a, b):
    return lax.dot_general(a, b, (((1,), (1,)), ((), ())), preferred_element_type=F32)


def prox_coef(value):
    return value - jnp.clip(value, -l1_weight, l1_weight)


def prox_share(share, dual, targets):
    resid = share - dual - targets
    return targets + resid - jnp.clip(resid / 2.0, -huber_width, huber_width)


class Plan:
    def __init__(self, axis, size, order):
        self.axis, self.size, self.order = axis, size, order
        self.levels = len(order) - 1
        self.chunks = 1 << self.levels

    def key(self):
        index = lax.axis_index(self.axis)
        key = 0
        for level in range(self.levels):
            bit = lax.rem(lax.div(index, 1 << self.order[level]), 2)
            key = key + bit * (1 << (self.levels - 1 - level))
        return key

    def place(self, location, key):
        out = 0
        for bit in range(self.levels):
            own = lax.rem(lax.div(key, 1 << bit), 2)
            out = out + ((1 - own) if (location >> bit) & 1 else own) * (1 << bit)
        return out

    def permute(self, value, bit):
        return lax.ppermute(value, self.axis, [(i, i ^ (1 << bit)) for i in range(self.size)])


class Sum:
    def __init__(self, plan, keep, send):
        self.plan, self.step = plan, 0
        self.current, self.halves = None, (keep, send)
        self.flying = plan.permute(send, plan.order[0]) if plan.levels else None

    def steps(self):
        return 2 * self.plan.levels + 1

    def advance(self, after=None):
        plan, levels = self.plan, self.plan.levels
        arrived = self.flying
        if after is not None:
            arrived, _ = lax.optimization_barrier((arrived, after))
        if self.step < levels:
            self.current = self.halves[0] + arrived
            nxt = self.step + 1
            if nxt < levels:
                half = self.current.shape[0] // 2
                self.halves = (self.current[:half], self.current[half:])
                self.flying = plan.permute(self.halves[1], plan.order[nxt])
            else:
                self.flying = plan.permute(self.current, plan.order[levels])
        else:
            if self.step == levels:
                self.current = self.current + arrived
            else:
                self.current = jnp.concatenate([self.current, arrived], axis=0)
            level = 2 * levels - 1 - self.step
            self.flying = plan.permute(self.current, plan.order[level])
        self.step += 1
        return self.current

    def result(self):
        return self.current, self.flying


def run_sums(waves, feat, last):
    rounds = waves[0][0].steps() - 1
    extra = feat.steps() - 1
    for turn in range(rounds):
        after = [one.advance(last if turn == 0 else None) for wave in waves for one in wave]
        goal = extra if turn + 1 == rounds else extra * (turn + 1) // rounds
        while feat.step < goal:
            feat.advance(after if turn + 1 == rounds else None)
    return [one.result() for wave in waves for one in wave], feat.result()


class Sizes:
    def __init__(self, mesh_shape, data_shape, cols):
        self.n_samp, self.n_feat = mesh_shape["samp"], mesh_shape["feat"]
        self.rows, self.feats = data_shape
        self.cols = cols
        bits = (self.n_samp - 1).bit_length()
        order = list(range(bits))
        self.colors = [
            Plan("samp", self.n_samp, order[n % bits:] + order[: n % bits]) for n in range(2 * HALVES)
        ]
        self.feat_plan = Plan("feat", self.n_feat, list(range((self.n_feat - 1).bit_length())))
        self.color_rows = self.feats // len(self.colors)
        self.half_rows = self.feats // HALVES
        self.coef_chunk = self.color_rows // self.colors[0].chunks
        self.share_chunk = self.rows // self.feat_plan.chunks
        self.own = self.rows // self.n_feat
        self.row_block = min(256, self.rows)
        self.feat_block = min(256, self.feats)


def coef_places(sz, half):
    out = []
    for color in range(2):
        plan = sz.colors[2 * half + color]
        key = plan.key()
        for location in range(plan.chunks):
            offset = color * sz.color_rows + plan.place(location, key) * sz.coef_chunk
            out.append((color, location, pl.multiple_of(offset, 8)))
    return out


def share_places(sz):
    key = sz.feat_plan.key()
    return [
        (location, pl.multiple_of(sz.feat_plan.place(location, key) * sz.share_chunk, 8))
        for location in range(sz.feat_plan.chunks)
    ]


def half_of(location, chunks, chunk_rows):
    half = chunks // 2
    return location // half, (location % half) * chunk_rows


def put_split(target, rows, cols, value):
    high, low = split(value)
    target[rows, :cols] = high
    target[rows, cols:] = low


def put_wide(wide_t, cols, value):
    high, low = split(value.T)
    wide_t[:cols, :] = high
    wide_t[cols:, :] = low


def triple(a_hi, a_lo, rows, value2, cols):
    wide = dot_nn(a_hi[rows, :], value2[...])
    return wide[:, :cols] + wide[:, cols:] + dot_nn(a_lo[rows, :], value2[:, :cols])


def chebyshev_steps(sz, g_hi, g_lo, resid, search, search2, total, part):
    theta, pairs = chebyshev_coefs()
    cols, block = sz.cols, sz.row_block
    blocks = [pl.ds(r * block, block) for r in range(sz.rows // block)]
    for rows in blocks:
        first = resid[rows, :] * (1.0 / theta)
        search[rows, :] = first
        total[rows, :] = first
        put_split(search2.at[0], rows, cols, first)
    for step in range(CHEB):
        last = step + 1 == CHEB
        now, later = search2.at[step % 2], search2.at[(step + 1) % 2]
        for rows in blocks:
            prod = triple(g_hi, g_lo, rows, now, cols)
            if step == 0:
                part[rows, :] = prod
            else:
                part[rows, :] += prod
            if not last:
                c_old, c_res = pairs[step]
                old = search[rows, :]
                res = resid[rows, :] - old - prod
                new = c_old * old + c_res * res
                resid[rows, :] = res
                search[rows, :] = new
                total[rows, :] += new
                put_split(later, rows, cols, new)


def spread_kernel(half, sz, wide_t, a_hi, a_lo, start, dual, keep0, keep1, send0, send1, plus, proj):
    cols, block = sz.cols, min(sz.feat_block, sz.half_rows)
    base = half * sz.half_rows
    for f in range(sz.half_rows // block):
        columns = pl.ds(base + f * block, block)
        rows = pl.ds(f * block, block)
        wide = dot_nn(wide_t[...], a_hi[:, columns])
        out = wide[:cols] + wide[cols:] + dot_nn(wide_t[:cols, :], a_lo[:, columns])
        source = columns if start.shape[0] == sz.feats else rows
        value = start[source, :] + out.T
        proj[rows, :] = value
        plus[rows, :] = dual[source, :] + value
    for color, location, offset in coef_places(sz, half):
        which, row = half_of(location, sz.colors[0].chunks, sz.coef_chunk)
        target = ((keep0, keep1), (send0, send1))[which][color]
        target[pl.ds(row, sz.coef_chunk), :] = proj[pl.ds(offset, sz.coef_chunk), :]


def emit_share(sz, scratch, half_share, keep, send):
    own = pl.ds(pl.multiple_of(lax.axis_index("feat") * sz.own, 8), sz.own)
    scratch[own, :] = scratch[own, :] - half_share
    for location, offset in share_places(sz):
        which, row = half_of(location, sz.feat_plan.chunks, sz.share_chunk)
        target = (keep, send)[which]
        target[pl.ds(row, sz.share_chunk), :] = scratch[pl.ds(offset, sz.share_chunk), :]


def first_kernel(sz, data, coef_in, tile_dual_in, share_dual_in, tile_share_in, share_in, targets_in,
                 a_hi, a_lo, g_hi, g_lo, start, wide_t, keep_s, send_s, out_sum,
                 a32, coef, tile_dual, share_dual, tile_share, share, targets,
                 start2, resid, search, search2, total, part, a_sem, in_sem):
    cols, block = sz.cols, sz.row_block
    blocks = sz.rows // block
    loads = []
    for r in range(blocks):
        rows = pl.ds(r * block, block)
        loads.append(pltpu.make_async_copy(data.at[rows, :], a32.at[rows, :], a_sem.at[r]))
    smalls = [
        pltpu.make_async_copy(src, dst, in_sem.at[n]) for n, (src, dst) in enumerate((
            (coef_in, coef), (tile_dual_in, tile_dual), (share_dual_in, share_dual),
            (tile_share_in, tile_share), (share_in, share), (targets_in, targets)))
    ]
    for copy in loads + smalls:
        copy.start()
    for r in range(blocks):
        rows = pl.ds(r * block, block)
        loads[r].wait()
        high, low = split(a32[rows, :])
        a_hi[rows, :] = high
        a_lo[rows, :] = low
        for c in range(r + 1):
            others = pl.ds(c * block, block)
            gram = dot_nt(a_hi[rows, :], a_hi[others, :])
            cross = dot_nt(a_hi[rows, :], a_lo[others, :])
            if c == r:
                gram = 0.5 * gram + cross
                gram = gram + gram.T
            else:
                gram = gram + cross + dot_nt(a_lo[rows, :], a_hi[others, :])
            high, low = split(gram)
            g_hi[rows, others] = high
            g_lo[rows, others] = low
            if c != r:
                high, low = split(gram.T)
                g_hi[others, rows] = high
                g_lo[others, rows] = low
    for copy in smalls:
        copy.wait()
    first = coef[...] - tile_dual[...]
    start[...] = first
    put_split(start2, slice(None), cols, first)
    for r in range(blocks):
        rows = pl.ds(r * block, block)
        prod = triple(a_hi, a_lo, rows, start2, cols)
        out_sum[rows, :] = prod
        resid[rows, :] = tile_share[rows, :] + share_dual[rows, :] - prod
    chebyshev_steps(sz, g_hi, g_lo, resid, search, search2, total, part)
    put_wide(wide_t, cols, total[...])
    part[...] += out_sum[...]
    out_sum[...] = part[...] + share_dual[...]
    own = pl.ds(pl.multiple_of(lax.axis_index("feat") * sz.own, 8), sz.own)
    half_share = prox_share(share[...], share_dual[own, :], targets[...])
    emit_share(sz, part, half_share, keep_s, send_s)


def update_kernel(half, sz, *refs):
    before = refs[9:10] if half else ()
    a_hi, a_lo, sum00, sum01, sum10, sum11, coef, coef_dual, dual_plus = refs[:9]
    start, tile_now, half_out, coef_plus, prod, start2 = refs[9 + len(before):]
    cols, block = sz.cols, sz.row_block
    base = half * sz.half_rows
    sums = ((sum00, sum01), (sum10, sum11))
    for color, location, offset in coef_places(sz, half):
        rows = pl.ds(offset, sz.coef_chunk)
        whole = pl.ds(base + offset, sz.coef_chunk)
        which, row = half_of(location, sz.colors[0].chunks, sz.coef_chunk)
        total_coef = sums[color][which][pl.ds(row, sz.coef_chunk), :]
        dual = coef_dual[whole, :]
        prox = prox_coef(coef[whole, :] - dual)
        new = (prox + total_coef) / (sz.n_samp + 1)
        dual = dual + prox - new
        prox = prox_coef(new - dual)
        half_out[rows, :] = prox
        coef_plus[rows, :] = dual + prox
        tile = dual_plus[rows, :] - new
        tile_now[rows, :] = tile
        start[rows, :] = new - tile
    put_split(start2, slice(None), cols, start[...])
    columns = pl.ds(base, sz.half_rows)
    for r in range(sz.rows // block):
        rows = pl.ds(r * block, block)
        wide = dot_nn(a_hi[rows, columns], start2[...])
        value = wide[:, :cols] + wide[:, cols:] + dot_nn(a_lo[rows, columns], start2[:, :cols])
        prod[rows, :] = value + before[0][rows, :] if half else value


def second_kernel(sz, g_hi, g_lo, prod, esum0, esum1, out_sum, targets, share, share_dual,
                  wide_t, keep_s, send_s, half_share_out, share_dual_out, proj_share,
                  resid, search, search2, total, part):
    esums = (esum0, esum1)
    for location, offset in share_places(sz):
        rows = pl.ds(offset, sz.share_chunk)
        which, row = half_of(location, sz.feat_plan.chunks, sz.share_chunk)
        excess = esums[which][pl.ds(row, sz.share_chunk), :] * (-1.0 / (sz.n_feat + 1))
        search[rows, :] = excess
        share_dual_out[rows, :] = share_dual[rows, :] + excess
        resid[rows, :] = out_sum[rows, :] + 2.0 * excess - prod[rows, :]
    own = pl.ds(pl.multiple_of(lax.axis_index("feat") * sz.own, 8), sz.own)
    share_now = prox_share(share[...], share_dual[own, :], targets[...]) - search[own, :]
    half_share = prox_share(share_now, share_dual_out[own, :], targets[...])
    half_share_out[...] = half_share
    chebyshev_steps(sz, g_hi, g_lo, resid, search, search2, total, part)
    put_wide(wide_t, sz.cols, total[...])
    part[...] += prod[...]
    proj_share[...] = part[...]
    emit_share(sz, part, half_share, keep_s, send_s)


def last_kernel(sz, *refs):
    coef_out, coef_dual_out, tile_out, share_out, share_dual_out, tile_share_out = refs[-6:]
    for half in range(HALVES):
        sum00, sum01, sum10, sum11, half_coef, coef_plus, tile_plus = refs[7 * half:7 * half + 7]
        sums = ((sum00, sum01), (sum10, sum11))
        for color, location, offset in coef_places(sz, half):
            rows = pl.ds(offset, sz.coef_chunk)
            whole = pl.ds(half * sz.half_rows + offset, sz.coef_chunk)
            which, row = half_of(location, sz.colors[0].chunks, sz.coef_chunk)
            total_coef = sums[color][which][pl.ds(row, sz.coef_chunk), :]
            new = (half_coef[rows, :] + total_coef) / (sz.n_samp + 1)
            coef_out[whole, :] = new
            coef_dual_out[whole, :] = coef_plus[rows, :] - new
            tile_out[whole, :] = tile_plus[rows, :] - new
    *esums, half_share, share_dual, proj_share = refs[7 * HALVES:7 * HALVES + 5]
    for location, offset in share_places(sz):
        rows = pl.ds(offset, sz.share_chunk)
        which, row = half_of(location, sz.feat_plan.chunks, sz.share_chunk)
        excess = esums[which][pl.ds(row, sz.share_chunk), :] * (-1.0 / (sz.n_feat + 1))
        share_dual_out[rows, :] = share_dual[rows, :] + excess
        tile_share_out[rows, :] = proj_share[rows, :] + excess
    own = pl.ds(pl.multiple_of(lax.axis_index("feat") * sz.own, 8), sz.own)
    share_out[...] = half_share[...] - (share_dual_out[own, :] - share_dual[own, :])


def shards(mesh_shape, data, targets, coef, coef_dual, tile_coef_dual, share, share_dual, tile_share):
    cols = coef.shape[1]
    sz = Sizes(mesh_shape, data.shape, cols)
    rows, feats = data.shape
    blocks = rows // sz.row_block
    f32 = lambda *shape: jax.ShapeDtypeStruct(shape, F32)
    v32 = lambda *shape: pltpu.VMEM(shape, F32)
    v16 = lambda *shape: pltpu.VMEM(shape, BF16)
    flops = 2 * rows * feats * cols

    def kernel(body, name, outs, scratch, work, limit, *operands, streamed=0):
        vmem = pl.BlockSpec(memory_space=pltpu.VMEM)
        hbm = pl.BlockSpec(memory_space=pltpu.HBM)
        operands = [
            pltpu.with_memory_space_constraint(x, pltpu.HBM) if n < streamed else x
            for n, x in enumerate(operands)
        ]
        return pl.pallas_call(
            body,
            out_shape=outs,
            in_specs=[hbm] * streamed + [vmem] * (len(operands) - streamed),
            out_specs=[vmem] * len(outs),
            scratch_shapes=scratch,
            compiler_params=pltpu.CompilerParams(vmem_limit_bytes=limit * MIB),
            cost_estimate=pl.CostEstimate(flops=work, bytes_accessed=8 * MIB, transcendentals=0),
            name=name,
        )(*operands)

    coef_sends = [v32(sz.color_rows // 2, cols)] * 4
    share_sends = [v32(rows // 2, cols)] * 2
    matrices = [v16(rows, feats)] * 2 + [v16(rows, rows)] * 2
    vector = v32(rows, cols)
    half_coefs = v32(sz.half_rows, cols)
    wide_t = v16(2 * cols, rows)
    work = [vector, vector, v16(2, rows, 2 * cols), vector, vector]
    tile_dual = tile_coef_dual[0]

    def project(wide, keep_s, send_s, starts, duals):
        feat = Sum(sz.feat_plan, keep_s, send_s)
        waves, pluses = [], []
        for half in range(HALVES):
            if half:
                wide, _ = lax.optimization_barrier((wide, pluses[-1]))
            keep0, keep1, send0, send1, plus = kernel(
                functools.partial(spread_kernel, half, sz), f"spread{half}", coef_sends + [half_coefs],
                [half_coefs], 3 * flops // HALVES, LIMIT, wide, a_hi, a_lo, starts[half], duals[half])
            pluses.append(plus)
            waves.append([
                Sum(sz.colors[2 * half], keep0, send0), Sum(sz.colors[2 * half + 1], keep1, send1)])
        feat.advance()
        sums, esums = run_sums(waves, feat, pluses[-1])
        groups = [sums[2 * half] + sums[2 * half + 1] for half in range(HALVES)]
        return groups, esums, pluses

    a_hi, a_lo, g_hi, g_lo, start, wide, keep_s, send_s, out_sum = kernel(
        functools.partial(first_kernel, sz), "first",
        matrices + [v32(feats, cols), wide_t] + share_sends + [vector],
        [v32(rows, feats), v32(feats, cols), v32(feats, cols), vector, vector, v32(sz.own, cols),
         v32(sz.own, cols), v16(feats, 2 * cols)] + work
        + [pltpu.SemaphoreType.DMA((blocks,)), pltpu.SemaphoreType.DMA((6,))], 30 * flops, 24,
        data, coef, tile_dual, share_dual, tile_share[0], share, targets, streamed=7)
    groups, esums, pluses = project(wide, keep_s, send_s, [start] * HALVES, [tile_dual] * HALVES)
    starts, duals, saved, prod = [], [], [], []
    for half in range(HALVES):
        start, tile_now, half_coef, coef_plus, total = kernel(
            functools.partial(update_kernel, half, sz), f"update{half}", [half_coefs] * 4 + [vector],
            [v16(sz.half_rows, 2 * cols)], 2 * flops // HALVES, LIMIT,
            a_hi, a_lo, *groups[half], coef, coef_dual, pluses[half], *prod)
        starts.append(start)
        duals.append(tile_now)
        saved.append((half_coef, coef_plus))
        prod = [total]
    wide, keep_s, send_s, half_share, dual_now, proj_share = kernel(
        functools.partial(second_kernel, sz), "second",
        [wide_t] + share_sends + [v32(sz.own, cols), vector, vector],
        work, 11 * flops, LIMIT, g_hi, g_lo, *prod, *esums, out_sum, targets, share, share_dual)
    groups, esums, pluses = project(wide, keep_s, send_s, starts, duals)
    halves = []
    for half in range(HALVES):
        halves += [*groups[half], *saved[half], pluses[half]]
    coef_out, coef_dual_out, tile_out, share_out, share_dual_out, tile_share_out = kernel(
        functools.partial(last_kernel, sz), "last",
        [f32(feats, cols)] * 3 + [f32(sz.own, cols), f32(rows, cols), f32(rows, cols)],
        [], flops // 100, LIMIT, *halves, *esums, half_share, dual_now, proj_share)
    return (coef_out, coef_dual_out, tile_out[None], share_out, share_dual_out, tile_share_out[None])


def solution(mesh):
    mesh_shape = dict(mesh.shape)
    return jax.shard_map(
        functools.partial(shards, mesh_shape),
        mesh=mesh,
        in_specs=(
            P("samp", "feat"),
            P(("samp", "feat"), None),
            P("feat", None),
            P("feat", None),
            P("samp", "feat", None),
            P(("samp", "feat"), None),
            P("samp", None),
            P("feat", "samp", None),
        ),
        out_specs=(
            P("feat", None),
            P("feat", None),
            P("samp", "feat", None),
            P(("samp", "feat"), None),
            P("samp", None),
            P("feat", "samp", None),
        ),
        check_vma=False,
    )
```

```python
import functools

import jax
import jax.numpy as jnp
from jax import lax
from jax.experimental import pallas as pl
from jax.experimental.pallas import tpu as pltpu
from jax.sharding import PartitionSpec as P

CHEB = 5

cheb_low = 1.0
cheb_high = 3.2
l1_weight = 0.2
huber_width = 4.0

F32 = jnp.float32
BF16 = jnp.bfloat16
MIB = 1 << 20
LIMIT = 16
HALVES = 2
ADD_FLOPS = 4 * 10**9


def chebyshev_coefs():
    theta = (cheb_high + cheb_low) / 2.0
    delta = (cheb_high - cheb_low) / 2.0
    sigma = theta / delta
    rho = 1.0 / sigma
    pairs = []
    for _ in range(CHEB - 1):
        rho_new = 1.0 / (2.0 * sigma - rho)
        pairs.append((rho_new * rho, 2.0 * rho_new / delta))
        rho = rho_new
    return theta, pairs


def split(value):
    high = value.astype(BF16)
    return high, (value - high.astype(F32)).astype(BF16)


def dot_nn(a, b):
    return jnp.dot(a, b, preferred_element_type=F32)


def dot_nt(a, b):
    return lax.dot_general(a, b, (((1,), (1,)), ((), ())), preferred_element_type=F32)


def prox_coef(value):
    return value - jnp.clip(value, -l1_weight, l1_weight)


def prox_share(share, dual, targets):
    resid = share - dual - targets
    return targets + resid - jnp.clip(resid / 2.0, -huber_width, huber_width)


class Plan:
    def __init__(self, axis, size, order):
        self.axis, self.size, self.order = axis, size, order
        self.levels = len(order) - 1
        self.chunks = 1 << self.levels

    def key(self):
        index = lax.axis_index(self.axis)
        key = 0
        for level in range(self.levels):
            bit = lax.rem(lax.div(index, 1 << self.order[level]), 2)
            key = key + bit * (1 << (self.levels - 1 - level))
        return key

    def place(self, location, key):
        out = 0
        for bit in range(self.levels):
            own = lax.rem(lax.div(key, 1 << bit), 2)
            out = out + ((1 - own) if (location >> bit) & 1 else own) * (1 << bit)
        return out

    def permute(self, value, bit):
        return lax.ppermute(value, self.axis, [(i, i ^ (1 << bit)) for i in range(self.size)])


class Sum:
    def __init__(self, plan, keep, send):
        self.plan, self.step = plan, 0
        self.current, self.halves = None, (keep, send)
        self.flying = plan.permute(send, plan.order[0]) if plan.levels else None

    def steps(self):
        return 2 * self.plan.levels + 1

    def terms(self):
        own = self.halves[0] if self.step < self.plan.levels else self.current
        return (own, self.flying) if self.step <= self.plan.levels else None

    def advance(self, total=None):
        plan, levels = self.plan, self.plan.levels
        if self.step <= levels:
            own, arrived = self.terms()
            self.current = own + arrived if total is None else total
        else:
            self.current = jnp.concatenate([self.current, self.flying], axis=0)
        nxt = self.step + 1
        if nxt < levels:
            half = self.current.shape[0] // 2
            self.halves = (self.current[:half], self.current[half:])
            self.flying = plan.permute(self.halves[1], plan.order[nxt])
        else:
            self.flying = plan.permute(self.current, plan.order[2 * levels - nxt if nxt > levels else levels])
        self.step = nxt


    def wait_for(self, after):
        self.flying, _ = lax.optimization_barrier((self.flying, after))

    def result(self):
        return self.current, self.flying


def add_kernel(*refs):
    count = len(refs) // 3
    for n in range(count):
        refs[2 * count + n][...] = refs[2 * n][...] + refs[2 * n + 1][...]


def add_all(pairs):
    vmem = pl.BlockSpec(memory_space=pltpu.VMEM)
    return pl.pallas_call(
        add_kernel,
        out_shape=[pltpu.VMEM(own.shape, F32) for own, _ in pairs],
        in_specs=[vmem] * (2 * len(pairs)),
        out_specs=[vmem] * len(pairs),
        compiler_params=pltpu.CompilerParams(vmem_limit_bytes=LIMIT * MIB),
        cost_estimate=pl.CostEstimate(flops=ADD_FLOPS, bytes_accessed=MIB, transcendentals=0),
        name="sums",
    )(*[x for pair in pairs for x in pair])


def step_all(group, before):
    for one in group:
        one.wait_for(before)
    pairs = [one.terms() for one in group]
    totals = [None] * len(group) if None in pairs else add_all(pairs)
    for one, total in zip(group, totals):
        one.advance(total)
    return [one.current for one in group]


def run_sums(waves, feat, last):
    rounds = waves[0][0].steps() - 1
    extra = feat.steps() - 1
    before, turns = last, rounds * len(waves)
    for turn in range(turns):
        before = step_all(waves[turn % len(waves)], before)
        while feat.step < min(feat.plan.levels, -(-feat.plan.levels * (turn + 1) // (turns - 1))):
            before = step_all([feat], before)
    while feat.step < extra:
        before = step_all([feat], before)
    return [one.result() for wave in waves for one in wave], feat.result()


class Sizes:
    def __init__(self, mesh_shape, data_shape, cols):
        self.n_samp, self.n_feat = mesh_shape["samp"], mesh_shape["feat"]
        self.rows, self.feats = data_shape
        self.cols = cols
        bits = (self.n_samp - 1).bit_length()
        order = list(range(bits))
        self.colors = [
            Plan("samp", self.n_samp, order[n % bits:] + order[: n % bits]) for n in range(2 * HALVES)
        ]
        self.feat_plan = Plan("feat", self.n_feat, list(range((self.n_feat - 1).bit_length())))
        self.color_rows = self.feats // len(self.colors)
        self.half_rows = self.feats // HALVES
        self.coef_chunk = self.color_rows // self.colors[0].chunks
        self.share_chunk = self.rows // self.feat_plan.chunks
        self.own = self.rows // self.n_feat
        self.row_block = min(256, self.rows)
        self.feat_block = min(256, self.feats)


def coef_places(sz, half):
    out = []
    for color in range(2):
        plan = sz.colors[2 * half + color]
        key = plan.key()
        for location in range(plan.chunks):
            offset = color * sz.color_rows + plan.place(location, key) * sz.coef_chunk
            out.append((color, location, pl.multiple_of(offset, 8)))
    return out


def share_places(sz):
    key = sz.feat_plan.key()
    return [
        (location, pl.multiple_of(sz.feat_plan.place(location, key) * sz.share_chunk, 8))
        for location in range(sz.feat_plan.chunks)
    ]


def half_of(location, chunks, chunk_rows):
    half = chunks // 2
    return location // half, (location % half) * chunk_rows


def put_split(target, rows, cols, value):
    high, low = split(value)
    target[rows, :cols] = high
    target[rows, cols:] = low


def put_wide(wide_t, cols, value):
    high, low = split(value.T)
    wide_t[:cols, :] = high
    wide_t[cols:, :] = low


def triple(a_hi, a_lo, rows, value2, cols):
    wide = dot_nn(a_hi[rows, :], value2[...])
    return wide[:, :cols] + wide[:, cols:] + dot_nn(a_lo[rows, :], value2[:, :cols])


def chebyshev_steps(sz, g_hi, g_lo, resid, search, search2, total, part):
    theta, pairs = chebyshev_coefs()
    cols, block = sz.cols, sz.row_block
    blocks = [pl.ds(r * block, block) for r in range(sz.rows // block)]
    for rows in blocks:
        first = resid[rows, :] * (1.0 / theta)
        search[rows, :] = first
        total[rows, :] = first
        put_split(search2.at[0], rows, cols, first)
    for step in range(CHEB):
        last = step + 1 == CHEB
        now, later = search2.at[step % 2], search2.at[(step + 1) % 2]
        for rows in blocks:
            prod = triple(g_hi, g_lo, rows, now, cols)
            if step == 0:
                part[rows, :] = prod
            else:
                part[rows, :] += prod
            if not last:
                c_old, c_res = pairs[step]
                old = search[rows, :]
                res = resid[rows, :] - old - prod
                new = c_old * old + c_res * res
                resid[rows, :] = res
                search[rows, :] = new
                total[rows, :] += new
                put_split(later, rows, cols, new)


def spread_kernel(half, sz, wide_t, a_hi, a_lo, start, dual, keep0, keep1, send0, send1, plus, proj):
    cols, block = sz.cols, min(sz.feat_block, sz.half_rows)
    base = half * sz.half_rows
    for f in range(sz.half_rows // block):
        columns = pl.ds(base + f * block, block)
        rows = pl.ds(f * block, block)
        wide = dot_nn(wide_t[...], a_hi[:, columns])
        out = wide[:cols] + wide[cols:] + dot_nn(wide_t[:cols, :], a_lo[:, columns])
        source = columns if start.shape[0] == sz.feats else rows
        value = start[source, :] + out.T
        proj[rows, :] = value
        plus[rows, :] = dual[source, :] + value
    for color, location, offset in coef_places(sz, half):
        which, row = half_of(location, sz.colors[0].chunks, sz.coef_chunk)
        target = ((keep0, keep1), (send0, send1))[which][color]
        target[pl.ds(row, sz.coef_chunk), :] = proj[pl.ds(offset, sz.coef_chunk), :]


def emit_share(sz, scratch, half_share, keep, send):
    own = pl.ds(pl.multiple_of(lax.axis_index("feat") * sz.own, 8), sz.own)
    scratch[own, :] = scratch[own, :] - half_share
    for location, offset in share_places(sz):
        which, row = half_of(location, sz.feat_plan.chunks, sz.share_chunk)
        target = (keep, send)[which]
        target[pl.ds(row, sz.share_chunk), :] = scratch[pl.ds(offset, sz.share_chunk), :]


def first_kernel(sz, data, coef_in, tile_dual_in, share_dual_in, tile_share_in, share_in, targets_in,
                 a_hi, a_lo, g_hi, g_lo, start, wide_t, keep_s, send_s, out_sum,
                 a32, coef, tile_dual, share_dual, tile_share, share, targets,
                 start2, resid, search, search2, total, part, a_sem, in_sem):
    cols, block = sz.cols, sz.row_block
    blocks = sz.rows // block
    loads = []
    for r in range(blocks):
        rows = pl.ds(r * block, block)
        loads.append(pltpu.make_async_copy(data.at[rows, :], a32.at[rows, :], a_sem.at[r]))
    smalls = [
        pltpu.make_async_copy(src, dst, in_sem.at[n]) for n, (src, dst) in enumerate((
            (coef_in, coef), (tile_dual_in, tile_dual), (share_dual_in, share_dual),
            (tile_share_in, tile_share), (share_in, share), (targets_in, targets)))
    ]
    for copy in loads + smalls:
        copy.start()
    for r in range(blocks):
        rows = pl.ds(r * block, block)
        loads[r].wait()
        high, low = split(a32[rows, :])
        a_hi[rows, :] = high
        a_lo[rows, :] = low
        for c in range(r + 1):
            others = pl.ds(c * block, block)
            gram = dot_nt(a_hi[rows, :], a_hi[others, :])
            cross = dot_nt(a_hi[rows, :], a_lo[others, :])
            if c == r:
                gram = 0.5 * gram + cross
                gram = gram + gram.T
            else:
                gram = gram + cross + dot_nt(a_lo[rows, :], a_hi[others, :])
            high, low = split(gram)
            g_hi[rows, others] = high
            g_lo[rows, others] = low
            if c != r:
                high, low = split(gram.T)
                g_hi[others, rows] = high
                g_lo[others, rows] = low
    for copy in smalls:
        copy.wait()
    first = coef[...] - tile_dual[...]
    start[...] = first
    put_split(start2, slice(None), cols, first)
    for r in range(blocks):
        rows = pl.ds(r * block, block)
        prod = triple(a_hi, a_lo, rows, start2, cols)
        out_sum[rows, :] = prod
        resid[rows, :] = tile_share[rows, :] + share_dual[rows, :] - prod
    chebyshev_steps(sz, g_hi, g_lo, resid, search, search2, total, part)
    put_wide(wide_t, cols, total[...])
    part[...] += out_sum[...]
    out_sum[...] = part[...] + share_dual[...]
    own = pl.ds(pl.multiple_of(lax.axis_index("feat") * sz.own, 8), sz.own)
    half_share = prox_share(share[...], share_dual[own, :], targets[...])
    emit_share(sz, part, half_share, keep_s, send_s)


def update_kernel(half, sz, *refs):
    before = refs[9:10] if half else ()
    a_hi, a_lo, sum00, sum01, sum10, sum11, coef, coef_dual, dual_plus = refs[:9]
    start, tile_now, half_out, coef_plus, prod, start2 = refs[9 + len(before):]
    cols, block = sz.cols, sz.row_block
    base = half * sz.half_rows
    sums = ((sum00, sum01), (sum10, sum11))
    for color, location, offset in coef_places(sz, half):
        rows = pl.ds(offset, sz.coef_chunk)
        whole = pl.ds(base + offset, sz.coef_chunk)
        which, row = half_of(location, sz.colors[0].chunks, sz.coef_chunk)
        total_coef = sums[color][which][pl.ds(row, sz.coef_chunk), :]
        dual = coef_dual[whole, :]
        prox = prox_coef(coef[whole, :] - dual)
        new = (prox + total_coef) / (sz.n_samp + 1)
        dual = dual + prox - new
        prox = prox_coef(new - dual)
        half_out[rows, :] = prox
        coef_plus[rows, :] = dual + prox
        tile = dual_plus[rows, :] - new
        tile_now[rows, :] = tile
        start[rows, :] = new - tile
    put_split(start2, slice(None), cols, start[...])
    columns = pl.ds(base, sz.half_rows)
    for r in range(sz.rows // block):
        rows = pl.ds(r * block, block)
        wide = dot_nn(a_hi[rows, columns], start2[...])
        value = wide[:, :cols] + wide[:, cols:] + dot_nn(a_lo[rows, columns], start2[:, :cols])
        prod[rows, :] = value + before[0][rows, :] if half else value


def second_kernel(sz, g_hi, g_lo, prod, esum0, esum1, out_sum, targets, share, share_dual,
                  wide_t, keep_s, send_s, half_share_out, share_dual_out, proj_share,
                  resid, search, search2, total, part):
    esums = (esum0, esum1)
    for location, offset in share_places(sz):
        rows = pl.ds(offset, sz.share_chunk)
        which, row = half_of(location, sz.feat_plan.chunks, sz.share_chunk)
        excess = esums[which][pl.ds(row, sz.share_chunk), :] * (-1.0 / (sz.n_feat + 1))
        search[rows, :] = excess
        share_dual_out[rows, :] = share_dual[rows, :] + excess
        resid[rows, :] = out_sum[rows, :] + 2.0 * excess - prod[rows, :]
    own = pl.ds(pl.multiple_of(lax.axis_index("feat") * sz.own, 8), sz.own)
    share_now = prox_share(share[...], share_dual[own, :], targets[...]) - search[own, :]
    half_share = prox_share(share_now, share_dual_out[own, :], targets[...])
    half_share_out[...] = half_share
    chebyshev_steps(sz, g_hi, g_lo, resid, search, search2, total, part)
    put_wide(wide_t, sz.cols, total[...])
    part[...] += prod[...]
    proj_share[...] = part[...]
    emit_share(sz, part, half_share, keep_s, send_s)


def last_kernel(half, sz, *refs):
    sum00, sum01, sum10, sum11, half_coef, coef_plus, tile_plus = refs[-14:-7] if not half else refs[3:10]
    outs, (new_s, dual_s, tile_s), sems = refs[-7:-4], refs[-4:-1], refs[-1]
    sums = ((sum00, sum01), (sum10, sum11))
    for color, location, offset in coef_places(sz, half):
        rows = pl.ds(offset, sz.coef_chunk)
        which, row = half_of(location, sz.colors[0].chunks, sz.coef_chunk)
        total_coef = sums[color][which][pl.ds(row, sz.coef_chunk), :]
        new = (half_coef[rows, :] + total_coef) / (sz.n_samp + 1)
        new_s[rows, :] = new
        dual_s[rows, :] = coef_plus[rows, :] - new
        tile_s[rows, :] = tile_plus[rows, :] - new
    whole = pl.ds(half * sz.half_rows, sz.half_rows)
    copies = [
        pltpu.make_async_copy(src, out.at[whole, :], sems.at[n])
        for n, (src, out) in enumerate(zip((new_s, dual_s, tile_s), outs))
    ]
    for copy in copies:
        copy.start()
    for copy in copies:
        copy.wait()


def last_share_kernel(sz, *refs):
    share_out, share_dual_out, tile_share_out = refs[-3:]
    *esums, half_share, share_dual, proj_share = refs[:-3]
    for location, offset in share_places(sz):
        rows = pl.ds(offset, sz.share_chunk)
        which, row = half_of(location, sz.feat_plan.chunks, sz.share_chunk)
        excess = esums[which][pl.ds(row, sz.share_chunk), :] * (-1.0 / (sz.n_feat + 1))
        share_dual_out[rows, :] = share_dual[rows, :] + excess
        tile_share_out[rows, :] = proj_share[rows, :] + excess
    own = pl.ds(pl.multiple_of(lax.axis_index("feat") * sz.own, 8), sz.own)
    share_out[...] = half_share[...] - (share_dual_out[own, :] - share_dual[own, :])


def shards(mesh_shape, data, targets, coef, coef_dual, tile_coef_dual, share, share_dual, tile_share):
    cols = coef.shape[1]
    sz = Sizes(mesh_shape, data.shape, cols)
    rows, feats = data.shape
    blocks = rows // sz.row_block
    f32 = lambda *shape: jax.ShapeDtypeStruct(shape, F32)
    v32 = lambda *shape: pltpu.VMEM(shape, F32)
    v16 = lambda *shape: pltpu.VMEM(shape, BF16)
    flops = 2 * rows * feats * cols

    def kernel(body, name, outs, scratch, work, limit, *operands, streamed=0, stored=False):
        vmem = pl.BlockSpec(memory_space=pltpu.VMEM)
        hbm = pl.BlockSpec(memory_space=pltpu.HBM)
        operands = [
            pltpu.with_memory_space_constraint(x, pltpu.HBM) if n < streamed else x
            for n, x in enumerate(operands)
        ]
        return pl.pallas_call(
            body,
            out_shape=outs,
            in_specs=[hbm] * streamed + [vmem] * (len(operands) - streamed),
            out_specs=[hbm if stored else vmem] * len(outs),
            scratch_shapes=scratch,
            input_output_aliases={n: n for n in range(streamed)} if stored else {},
            compiler_params=pltpu.CompilerParams(vmem_limit_bytes=limit * MIB),
            cost_estimate=pl.CostEstimate(flops=work, bytes_accessed=8 * MIB, transcendentals=0),
            name=name,
        )(*operands)

    coef_sends = [v32(sz.color_rows // 2, cols)] * 4
    share_sends = [v32(rows // 2, cols)] * 2
    matrices = [v16(rows, feats)] * 2 + [v16(rows, rows)] * 2
    vector = v32(rows, cols)
    half_coefs = v32(sz.half_rows, cols)
    wide_t = v16(2 * cols, rows)
    work = [vector, vector, v16(2, rows, 2 * cols), vector, vector]
    tile_dual = tile_coef_dual[0]

    def project(wide, keep_s, send_s, starts, duals):
        feat = Sum(sz.feat_plan, keep_s, send_s)
        waves, pluses = [], []
        for half in range(HALVES):
            if half:
                wide, _ = lax.optimization_barrier((wide, pluses[-1]))
            keep0, keep1, send0, send1, plus = kernel(
                functools.partial(spread_kernel, half, sz), f"spread{half}", coef_sends + [half_coefs],
                [half_coefs], 3 * flops // HALVES, LIMIT, wide, a_hi, a_lo, starts[half], duals[half])
            pluses.append(plus)
            waves.append([
                Sum(sz.colors[2 * half], keep0, send0), Sum(sz.colors[2 * half + 1], keep1, send1)])
        sums, esums = run_sums(waves, feat, pluses[-1])
        groups = [sums[2 * half] + sums[2 * half + 1] for half in range(HALVES)]
        return groups, esums, pluses

    a_hi, a_lo, g_hi, g_lo, start, wide, keep_s, send_s, out_sum = kernel(
        functools.partial(first_kernel, sz), "first",
        matrices + [v32(feats, cols), wide_t] + share_sends + [vector],
        [v32(rows, feats), v32(feats, cols), v32(feats, cols), vector, vector, v32(sz.own, cols),
         v32(sz.own, cols), v16(feats, 2 * cols)] + work
        + [pltpu.SemaphoreType.DMA((blocks,)), pltpu.SemaphoreType.DMA((6,))], 30 * flops, 24,
        data, coef, tile_dual, share_dual, tile_share[0], share, targets, streamed=7)
    groups, esums, pluses = project(wide, keep_s, send_s, [start] * HALVES, [tile_dual] * HALVES)
    starts, duals, saved, prod = [], [], [], []
    for half in range(HALVES):
        start, tile_now, half_coef, coef_plus, total = kernel(
            functools.partial(update_kernel, half, sz), f"update{half}", [half_coefs] * 4 + [vector],
            [v16(sz.half_rows, 2 * cols)], 2 * ADD_FLOPS, LIMIT,
            a_hi, a_lo, *groups[half], coef, coef_dual, pluses[half], *prod)
        starts.append(start)
        duals.append(tile_now)
        saved.append((half_coef, coef_plus))
        prod = [total]
    wide, keep_s, send_s, half_share, dual_now, proj_share = kernel(
        functools.partial(second_kernel, sz), "second",
        [wide_t] + share_sends + [v32(sz.own, cols), vector, vector],
        work, 11 * flops, LIMIT, g_hi, g_lo, *prod, *esums, out_sum, targets, share, share_dual)
    groups, esums, pluses = project(wide, keep_s, send_s, starts, duals)
    finals = []
    for half in range(HALVES):
        finals = kernel(
            functools.partial(last_kernel, half, sz), f"last{half}", [f32(feats, cols)] * 3,
            [half_coefs] * 3 + [pltpu.SemaphoreType.DMA((3,))], 2 * ADD_FLOPS, LIMIT,
            *finals, *groups[half], *saved[half], pluses[half], streamed=len(finals), stored=True)
    coef_out, coef_dual_out, tile_out = finals
    share_out, share_dual_out, tile_share_out = kernel(
        functools.partial(last_share_kernel, sz), "last_share",
        [f32(sz.own, cols), f32(rows, cols), f32(rows, cols)],
        [], flops // 100, LIMIT, *esums, half_share, dual_now, proj_share)
    return (coef_out, coef_dual_out, tile_out[None], share_out, share_dual_out, tile_share_out[None])


def solution(mesh):
    mesh_shape = dict(mesh.shape)
    return jax.shard_map(
        functools.partial(shards, mesh_shape),
        mesh=mesh,
        in_specs=(
            P("samp", "feat"),
            P(("samp", "feat"), None),
            P("feat", None),
            P("feat", None),
            P("samp", "feat", None),
            P(("samp", "feat"), None),
            P("samp", None),
            P("feat", "samp", None),
        ),
        out_specs=(
            P("feat", None),
            P("feat", None),
            P("samp", "feat", None),
            P(("samp", "feat"), None),
            P("samp", None),
            P("feat", "samp", None),
        ),
        check_vma=False,
    )
```

```python
import functools

import jax
import jax.numpy as jnp
from jax import lax
from jax.experimental import pallas as pl
from jax.experimental.pallas import tpu as pltpu
from jax.sharding import PartitionSpec as P

CHEB = 5

cheb_low = 1.0
cheb_high = 3.2
l1_weight = 0.2
huber_width = 4.0

F32 = jnp.float32
BF16 = jnp.bfloat16
MIB = 1 << 20
LIMIT = 16
HALVES = 2
FULL_STEPS = 4
ADD_FLOPS = 4 * 10**9


def chebyshev_coefs():
    theta = (cheb_high + cheb_low) / 2.0
    delta = (cheb_high - cheb_low) / 2.0
    sigma = theta / delta
    rho = 1.0 / sigma
    pairs = []
    for _ in range(CHEB - 1):
        rho_new = 1.0 / (2.0 * sigma - rho)
        pairs.append((rho_new * rho, 2.0 * rho_new / delta))
        rho = rho_new
    return theta, pairs


def split(value):
    high = value.astype(BF16)
    return high, (value - high.astype(F32)).astype(BF16)


def dot_nn(a, b):
    return jnp.dot(a, b, preferred_element_type=F32)


def dot_nt(a, b):
    return lax.dot_general(a, b, (((1,), (1,)), ((), ())), preferred_element_type=F32)


def prox_coef(value):
    return value - jnp.clip(value, -l1_weight, l1_weight)


def prox_share(share, dual, targets):
    resid = share - dual - targets
    return targets + resid - jnp.clip(resid / 2.0, -huber_width, huber_width)


class Plan:
    def __init__(self, axis, size, order):
        self.axis, self.size, self.order = axis, size, order
        self.levels = len(order) - 1
        self.chunks = 1 << self.levels

    def key(self):
        index = lax.axis_index(self.axis)
        key = 0
        for level in range(self.levels):
            bit = lax.rem(lax.div(index, 1 << self.order[level]), 2)
            key = key + bit * (1 << (self.levels - 1 - level))
        return key

    def place(self, location, key):
        out = 0
        for bit in range(self.levels):
            own = lax.rem(lax.div(key, 1 << bit), 2)
            out = out + ((1 - own) if (location >> bit) & 1 else own) * (1 << bit)
        return out

    def permute(self, value, bit):
        return lax.ppermute(value, self.axis, [(i, i ^ (1 << bit)) for i in range(self.size)])


class Sum:
    def __init__(self, plan, keep, send):
        self.plan, self.step = plan, 0
        self.current, self.halves = None, (keep, send)
        self.flying = plan.permute(send, plan.order[0]) if plan.levels else None

    def steps(self):
        return 2 * self.plan.levels + 1

    def terms(self):
        own = self.halves[0] if self.step < self.plan.levels else self.current
        return (own, self.flying) if self.step <= self.plan.levels else None

    def advance(self, total=None):
        plan, levels = self.plan, self.plan.levels
        if self.step <= levels:
            own, arrived = self.terms()
            self.current = own + arrived if total is None else total
        else:
            self.current = jnp.concatenate([self.current, self.flying], axis=0)
        nxt = self.step + 1
        if nxt < levels:
            half = self.current.shape[0] // 2
            self.halves = (self.current[:half], self.current[half:])
            self.flying = plan.permute(self.halves[1], plan.order[nxt])
        else:
            self.flying = plan.permute(self.current, plan.order[2 * levels - nxt if nxt > levels else levels])
        self.step = nxt


    def wait_for(self, after):
        self.flying, _ = lax.optimization_barrier((self.flying, after))

    def result(self):
        return self.current, self.flying


def add_kernel(*refs):
    count = len(refs) // 3
    for n in range(count):
        refs[2 * count + n][...] = refs[2 * n][...] + refs[2 * n + 1][...]


def add_all(pairs):
    vmem = pl.BlockSpec(memory_space=pltpu.VMEM)
    return pl.pallas_call(
        add_kernel,
        out_shape=[pltpu.VMEM(own.shape, F32) for own, _ in pairs],
        in_specs=[vmem] * (2 * len(pairs)),
        out_specs=[vmem] * len(pairs),
        compiler_params=pltpu.CompilerParams(vmem_limit_bytes=LIMIT * MIB),
        cost_estimate=pl.CostEstimate(flops=ADD_FLOPS, bytes_accessed=MIB, transcendentals=0),
        name="sums",
    )(*[x for pair in pairs for x in pair])


def step_all(group, before):
    for one in group:
        one.wait_for(before)
    pairs = [one.terms() for one in group]
    totals = [None] * len(group) if None in pairs else add_all(pairs)
    for one, total in zip(group, totals):
        one.advance(total)
    return [one.current for one in group]


def run_sums(waves, feat, last):
    rounds = waves[0][0].steps() - 1
    extra = feat.steps() - 1
    before, turns = last, rounds * len(waves)
    for turn in range(turns):
        before = step_all(waves[turn % len(waves)], before)
        levels = feat.plan.levels
        while feat.step < 1 + min(levels, 1 + (levels - 1) * turn // (turns - 1)):
            before = step_all([feat], before)
    while feat.step < extra:
        before = step_all([feat], before)
    return [one.result() for wave in waves for one in wave], feat.result()


class Sizes:
    def __init__(self, mesh_shape, data_shape, cols):
        self.n_samp, self.n_feat = mesh_shape["samp"], mesh_shape["feat"]
        self.rows, self.feats = data_shape
        self.cols = cols
        bits = (self.n_samp - 1).bit_length()
        order = list(range(bits))
        self.colors = [
            Plan("samp", self.n_samp, order[n % bits:] + order[: n % bits]) for n in range(2 * HALVES)
        ]
        self.feat_plan = Plan("feat", self.n_feat, list(range((self.n_feat - 1).bit_length())))
        self.color_rows = self.feats // len(self.colors)
        self.half_rows = self.feats // HALVES
        self.coef_chunk = self.color_rows // self.colors[0].chunks
        self.share_chunk = self.rows // self.feat_plan.chunks
        self.own = self.rows // self.n_feat
        self.row_block = min(256, self.rows)
        self.feat_block = min(256, self.feats)


def coef_places(sz, half):
    out = []
    for color in range(2):
        plan = sz.colors[2 * half + color]
        key = plan.key()
        for location in range(plan.chunks):
            offset = color * sz.color_rows + plan.place(location, key) * sz.coef_chunk
            out.append((color, location, pl.multiple_of(offset, 8)))
    return out


def share_places(sz):
    key = sz.feat_plan.key()
    return [
        (location, pl.multiple_of(sz.feat_plan.place(location, key) * sz.share_chunk, 8))
        for location in range(sz.feat_plan.chunks)
    ]


def half_of(location, chunks, chunk_rows):
    half = chunks // 2
    return location // half, (location % half) * chunk_rows


def put_split(target, rows, cols, value):
    high, low = split(value)
    target[rows, :cols] = high
    target[rows, cols:] = low


def put_wide(wide_t, cols, value):
    high, low = split(value.T)
    wide_t[:cols, :] = high
    wide_t[cols:, :] = low


def triple(a_hi, a_lo, rows, value2, cols):
    wide = dot_nn(a_hi[rows, :], value2[...])
    return wide[:, :cols] + wide[:, cols:] + dot_nn(a_lo[rows, :], value2[:, :cols])


def chebyshev_steps(sz, g_hi, g_lo, resid, search, search2, total, part):
    theta, pairs = chebyshev_coefs()
    cols, block = sz.cols, sz.row_block
    blocks = [pl.ds(r * block, block) for r in range(sz.rows // block)]
    for rows in blocks:
        first = resid[rows, :] * (1.0 / theta)
        search[rows, :] = first
        total[rows, :] = first
        put_split(search2.at[0], rows, cols, first)
    for step in range(CHEB):
        last = step + 1 == CHEB
        now, later = search2.at[step % 2], search2.at[(step + 1) % 2]
        for rows in blocks:
            if step < FULL_STEPS:
                prod = triple(g_hi, g_lo, rows, now, cols)
            else:
                wide = dot_nn(g_hi[rows, :], now[...])
                prod = wide[:, :cols] + wide[:, cols:]
            if step == 0:
                part[rows, :] = prod
            else:
                part[rows, :] += prod
            if not last:
                c_old, c_res = pairs[step]
                old = search[rows, :]
                res = resid[rows, :] - old - prod
                new = c_old * old + c_res * res
                resid[rows, :] = res
                search[rows, :] = new
                total[rows, :] += new
                put_split(later, rows, cols, new)


def spread_kernel(half, sz, wide_t, a_hi, a_lo, start, dual, keep0, keep1, send0, send1, plus, proj):
    cols, block = sz.cols, min(sz.feat_block, sz.half_rows)
    base = half * sz.half_rows
    for f in range(sz.half_rows // block):
        columns = pl.ds(base + f * block, block)
        rows = pl.ds(f * block, block)
        wide = dot_nn(wide_t[...], a_hi[:, columns])
        out = wide[:cols] + wide[cols:] + dot_nn(wide_t[:cols, :], a_lo[:, columns])
        source = columns if start.shape[0] == sz.feats else rows
        value = start[source, :] + out.T
        proj[rows, :] = value
        plus[rows, :] = dual[source, :] + value
    for color, location, offset in coef_places(sz, half):
        which, row = half_of(location, sz.colors[0].chunks, sz.coef_chunk)
        target = ((keep0, keep1), (send0, send1))[which][color]
        target[pl.ds(row, sz.coef_chunk), :] = proj[pl.ds(offset, sz.coef_chunk), :]


def emit_share(sz, scratch, half_share, keep, send):
    own = pl.ds(pl.multiple_of(lax.axis_index("feat") * sz.own, 8), sz.own)
    scratch[own, :] = scratch[own, :] - half_share
    for location, offset in share_places(sz):
        which, row = half_of(location, sz.feat_plan.chunks, sz.share_chunk)
        target = (keep, send)[which]
        target[pl.ds(row, sz.share_chunk), :] = scratch[pl.ds(offset, sz.share_chunk), :]


def first_kernel(sz, data, coef_in, tile_dual_in, share_dual_in, tile_share_in, share_in, targets_in,
                 a_hi, a_lo, g_hi, g_lo, start, wide_t, keep_s, send_s, out_sum,
                 a32, coef, tile_dual, share_dual, tile_share, share, targets,
                 start2, resid, search, search2, total, part, a_sem, in_sem):
    cols, block = sz.cols, sz.row_block
    blocks = sz.rows // block
    loads = []
    for r in range(blocks):
        rows = pl.ds(r * block, block)
        loads.append(pltpu.make_async_copy(data.at[rows, :], a32.at[rows, :], a_sem.at[r]))
    smalls = [
        pltpu.make_async_copy(src, dst, in_sem.at[n]) for n, (src, dst) in enumerate((
            (coef_in, coef), (tile_dual_in, tile_dual), (share_dual_in, share_dual),
            (tile_share_in, tile_share), (share_in, share), (targets_in, targets)))
    ]
    for copy in loads + smalls:
        copy.start()
    for r in range(blocks):
        rows = pl.ds(r * block, block)
        loads[r].wait()
        high, low = split(a32[rows, :])
        a_hi[rows, :] = high
        a_lo[rows, :] = low
        for c in range(r + 1):
            others = pl.ds(c * block, block)
            gram = dot_nt(a_hi[rows, :], a_hi[others, :])
            cross = dot_nt(a_hi[rows, :], a_lo[others, :])
            if c == r:
                gram = 0.5 * gram + cross
                gram = gram + gram.T
            else:
                gram = gram + cross + dot_nt(a_lo[rows, :], a_hi[others, :])
            high, low = split(gram)
            g_hi[rows, others] = high
            g_lo[rows, others] = low
            if c != r:
                high, low = split(gram.T)
                g_hi[others, rows] = high
                g_lo[others, rows] = low
    for copy in smalls:
        copy.wait()
    first = coef[...] - tile_dual[...]
    start[...] = first
    put_split(start2, slice(None), cols, first)
    for r in range(blocks):
        rows = pl.ds(r * block, block)
        prod = triple(a_hi, a_lo, rows, start2, cols)
        out_sum[rows, :] = prod
        resid[rows, :] = tile_share[rows, :] + share_dual[rows, :] - prod
    chebyshev_steps(sz, g_hi, g_lo, resid, search, search2, total, part)
    put_wide(wide_t, cols, total[...])
    part[...] += out_sum[...]
    out_sum[...] = part[...] + share_dual[...]
    own = pl.ds(pl.multiple_of(lax.axis_index("feat") * sz.own, 8), sz.own)
    half_share = prox_share(share[...], share_dual[own, :], targets[...])
    emit_share(sz, part, half_share, keep_s, send_s)


def update_kernel(half, sz, *refs):
    before = refs[9:10] if half else ()
    a_hi, a_lo, sum00, sum01, sum10, sum11, coef, coef_dual, dual_plus = refs[:9]
    start, tile_now, half_out, coef_plus, prod, start2 = refs[9 + len(before):]
    cols, block = sz.cols, sz.row_block
    base = half * sz.half_rows
    sums = ((sum00, sum01), (sum10, sum11))
    for color, location, offset in coef_places(sz, half):
        rows = pl.ds(offset, sz.coef_chunk)
        whole = pl.ds(base + offset, sz.coef_chunk)
        which, row = half_of(location, sz.colors[0].chunks, sz.coef_chunk)
        total_coef = sums[color][which][pl.ds(row, sz.coef_chunk), :]
        dual = coef_dual[whole, :]
        prox = prox_coef(coef[whole, :] - dual)
        new = (prox + total_coef) / (sz.n_samp + 1)
        dual = dual + prox - new
        prox = prox_coef(new - dual)
        half_out[rows, :] = prox
        coef_plus[rows, :] = dual + prox
        tile = dual_plus[rows, :] - new
        tile_now[rows, :] = tile
        start[rows, :] = new - tile
    put_split(start2, slice(None), cols, start[...])
    columns = pl.ds(base, sz.half_rows)
    for r in range(sz.rows // block):
        rows = pl.ds(r * block, block)
        wide = dot_nn(a_hi[rows, columns], start2[...])
        value = wide[:, :cols] + wide[:, cols:] + dot_nn(a_lo[rows, columns], start2[:, :cols])
        prod[rows, :] = value + before[0][rows, :] if half else value


def second_kernel(sz, g_hi, g_lo, prod, esum0, esum1, out_sum, targets, share, share_dual,
                  wide_t, keep_s, send_s, half_share_out, share_dual_out, proj_share,
                  resid, search, search2, total, part):
    esums = (esum0, esum1)
    for location, offset in share_places(sz):
        rows = pl.ds(offset, sz.share_chunk)
        which, row = half_of(location, sz.feat_plan.chunks, sz.share_chunk)
        excess = esums[which][pl.ds(row, sz.share_chunk), :] * (-1.0 / (sz.n_feat + 1))
        search[rows, :] = excess
        share_dual_out[rows, :] = share_dual[rows, :] + excess
        resid[rows, :] = out_sum[rows, :] + 2.0 * excess - prod[rows, :]
    own = pl.ds(pl.multiple_of(lax.axis_index("feat") * sz.own, 8), sz.own)
    share_now = prox_share(share[...], share_dual[own, :], targets[...]) - search[own, :]
    half_share = prox_share(share_now, share_dual_out[own, :], targets[...])
    half_share_out[...] = half_share
    chebyshev_steps(sz, g_hi, g_lo, resid, search, search2, total, part)
    put_wide(wide_t, sz.cols, total[...])
    part[...] += prod[...]
    proj_share[...] = part[...]
    emit_share(sz, part, half_share, keep_s, send_s)


def last_kernel(half, sz, *refs):
    sum00, sum01, sum10, sum11, half_coef, coef_plus, tile_plus = refs[-14:-7] if not half else refs[3:10]
    outs, (new_s, dual_s, tile_s), sems = refs[-7:-4], refs[-4:-1], refs[-1]
    sums = ((sum00, sum01), (sum10, sum11))
    for color, location, offset in coef_places(sz, half):
        rows = pl.ds(offset, sz.coef_chunk)
        which, row = half_of(location, sz.colors[0].chunks, sz.coef_chunk)
        total_coef = sums[color][which][pl.ds(row, sz.coef_chunk), :]
        new = (half_coef[rows, :] + total_coef) / (sz.n_samp + 1)
        new_s[rows, :] = new
        dual_s[rows, :] = coef_plus[rows, :] - new
        tile_s[rows, :] = tile_plus[rows, :] - new
    whole = pl.ds(half * sz.half_rows, sz.half_rows)
    copies = [
        pltpu.make_async_copy(src, out.at[whole, :], sems.at[n])
        for n, (src, out) in enumerate(zip((new_s, dual_s, tile_s), outs))
    ]
    for copy in copies:
        copy.start()
    for copy in copies:
        copy.wait()


def last_share_kernel(sz, *refs):
    share_out, share_dual_out, tile_share_out = refs[-3:]
    *esums, half_share, share_dual, proj_share = refs[:-3]
    for location, offset in share_places(sz):
        rows = pl.ds(offset, sz.share_chunk)
        which, row = half_of(location, sz.feat_plan.chunks, sz.share_chunk)
        excess = esums[which][pl.ds(row, sz.share_chunk), :] * (-1.0 / (sz.n_feat + 1))
        share_dual_out[rows, :] = share_dual[rows, :] + excess
        tile_share_out[rows, :] = proj_share[rows, :] + excess
    own = pl.ds(pl.multiple_of(lax.axis_index("feat") * sz.own, 8), sz.own)
    share_out[...] = half_share[...] - (share_dual_out[own, :] - share_dual[own, :])


def shards(mesh_shape, data, targets, coef, coef_dual, tile_coef_dual, share, share_dual, tile_share):
    cols = coef.shape[1]
    sz = Sizes(mesh_shape, data.shape, cols)
    rows, feats = data.shape
    blocks = rows // sz.row_block
    f32 = lambda *shape: jax.ShapeDtypeStruct(shape, F32)
    v32 = lambda *shape: pltpu.VMEM(shape, F32)
    v16 = lambda *shape: pltpu.VMEM(shape, BF16)
    flops = 2 * rows * feats * cols

    def kernel(body, name, outs, scratch, work, limit, *operands, streamed=0, stored=False):
        vmem = pl.BlockSpec(memory_space=pltpu.VMEM)
        hbm = pl.BlockSpec(memory_space=pltpu.HBM)
        operands = [
            pltpu.with_memory_space_constraint(x, pltpu.HBM) if n < streamed else x
            for n, x in enumerate(operands)
        ]
        return pl.pallas_call(
            body,
            out_shape=outs,
            in_specs=[hbm] * streamed + [vmem] * (len(operands) - streamed),
            out_specs=[hbm if stored else vmem] * len(outs),
            scratch_shapes=scratch,
            input_output_aliases={n: n for n in range(streamed)} if stored else {},
            compiler_params=pltpu.CompilerParams(vmem_limit_bytes=limit * MIB),
            cost_estimate=pl.CostEstimate(flops=work, bytes_accessed=8 * MIB, transcendentals=0),
            name=name,
        )(*operands)

    coef_sends = [v32(sz.color_rows // 2, cols)] * 4
    share_sends = [v32(rows // 2, cols)] * 2
    matrices = [v16(rows, feats)] * 2 + [v16(rows, rows)] * 2
    vector = v32(rows, cols)
    half_coefs = v32(sz.half_rows, cols)
    wide_t = v16(2 * cols, rows)
    work = [vector, vector, v16(2, rows, 2 * cols), vector, vector]
    tile_dual = tile_coef_dual[0]

    def project(wide, keep_s, send_s, starts, duals, early):
        feat = Sum(sz.feat_plan, keep_s, send_s)
        waves, pluses = [], []
        for half in range(HALVES):
            if half:
                wide, _ = lax.optimization_barrier((wide, step_all([feat], pluses[-1]) if early else pluses[-1]))
            keep0, keep1, send0, send1, plus = kernel(
                functools.partial(spread_kernel, half, sz), f"spread{half}", coef_sends + [half_coefs],
                [half_coefs], 3 * flops // HALVES, LIMIT, wide, a_hi, a_lo, starts[half], duals[half])
            pluses.append(plus)
            waves.append([
                Sum(sz.colors[2 * half], keep0, send0), Sum(sz.colors[2 * half + 1], keep1, send1)])
        sums, esums = run_sums(waves, feat, pluses[-1] if early else step_all([feat], pluses[-1]))
        groups = [sums[2 * half] + sums[2 * half + 1] for half in range(HALVES)]
        return groups, esums, pluses

    a_hi, a_lo, g_hi, g_lo, start, wide, keep_s, send_s, out_sum = kernel(
        functools.partial(first_kernel, sz), "first",
        matrices + [v32(feats, cols), wide_t] + share_sends + [vector],
        [v32(rows, feats), v32(feats, cols), v32(feats, cols), vector, vector, v32(sz.own, cols),
         v32(sz.own, cols), v16(feats, 2 * cols)] + work
        + [pltpu.SemaphoreType.DMA((blocks,)), pltpu.SemaphoreType.DMA((6,))], 30 * flops, 24,
        data, coef, tile_dual, share_dual, tile_share[0], share, targets, streamed=7)
    groups, esums, pluses = project(wide, keep_s, send_s, [start] * HALVES, [tile_dual] * HALVES, True)
    starts, duals, saved, prod = [], [], [], []
    for half in range(HALVES):
        start, tile_now, half_coef, coef_plus, total = kernel(
            functools.partial(update_kernel, half, sz), f"update{half}", [half_coefs] * 4 + [vector],
            [v16(sz.half_rows, 2 * cols)], 2 * ADD_FLOPS, LIMIT,
            a_hi, a_lo, *groups[half], coef, coef_dual, pluses[half], *prod)
        starts.append(start)
        duals.append(tile_now)
        saved.append((half_coef, coef_plus))
        prod = [total]
    wide, keep_s, send_s, half_share, dual_now, proj_share = kernel(
        functools.partial(second_kernel, sz), "second",
        [wide_t] + share_sends + [v32(sz.own, cols), vector, vector],
        work, 11 * flops, LIMIT, g_hi, g_lo, *prod, *esums, out_sum, targets, share, share_dual)
    groups, esums, pluses = project(wide, keep_s, send_s, starts, duals, False)
    finals = []
    for half in range(HALVES):
        finals = kernel(
            functools.partial(last_kernel, half, sz), f"last{half}", [f32(feats, cols)] * 3,
            [half_coefs] * 3 + [pltpu.SemaphoreType.DMA((3,))], 2 * ADD_FLOPS, LIMIT,
            *finals, *groups[half], *saved[half], pluses[half], streamed=len(finals), stored=True)
    coef_out, coef_dual_out, tile_out = finals
    share_out, share_dual_out, tile_share_out = kernel(
        functools.partial(last_share_kernel, sz), "last_share",
        [f32(sz.own, cols), f32(rows, cols), f32(rows, cols)],
        [], flops // 100, LIMIT, *esums, half_share, dual_now, proj_share)
    return (coef_out, coef_dual_out, tile_out[None], share_out, share_dual_out, tile_share_out[None])


def solution(mesh):
    mesh_shape = dict(mesh.shape)
    return jax.shard_map(
        functools.partial(shards, mesh_shape),
        mesh=mesh,
        in_specs=(
            P("samp", "feat"),
            P(("samp", "feat"), None),
            P("feat", None),
            P("feat", None),
            P("samp", "feat", None),
            P(("samp", "feat"), None),
            P("samp", None),
            P("feat", "samp", None),
        ),
        out_specs=(
            P("feat", None),
            P("feat", None),
            P("samp", "feat", None),
            P(("samp", "feat"), None),
            P("samp", None),
            P("feat", "samp", None),
        ),
        check_vma=False,
    )
```

```python
import functools

import jax
import jax.numpy as jnp
from jax import lax
from jax.experimental import pallas as pl
from jax.experimental.pallas import tpu as pltpu
from jax.sharding import PartitionSpec as P

CHEB = 5

cheb_low = 1.0
cheb_high = 3.2
l1_weight = 0.2
huber_width = 4.0

F32 = jnp.float32
BF16 = jnp.bfloat16
MIB = 1 << 20
LIMIT = 16
HALVES = 2
FULL_STEPS = 4
ADD_FLOPS = 4 * 10**9


def chebyshev_coefs():
    theta = (cheb_high + cheb_low) / 2.0
    delta = (cheb_high - cheb_low) / 2.0
    sigma = theta / delta
    rho = 1.0 / sigma
    pairs = []
    for _ in range(CHEB - 1):
        rho_new = 1.0 / (2.0 * sigma - rho)
        pairs.append((rho_new * rho, 2.0 * rho_new / delta))
        rho = rho_new
    return theta, pairs


def split(value):
    high = value.astype(BF16)
    return high, (value - high.astype(F32)).astype(BF16)


def dot_nn(a, b):
    return jnp.dot(a, b, preferred_element_type=F32)


def dot_nt(a, b):
    return lax.dot_general(a, b, (((1,), (1,)), ((), ())), preferred_element_type=F32)


def prox_coef(value):
    return value - jnp.clip(value, -l1_weight, l1_weight)


def prox_share(share, dual, targets):
    resid = share - dual - targets
    return targets + resid - jnp.clip(resid / 2.0, -huber_width, huber_width)


class Plan:
    def __init__(self, axis, size, order):
        self.axis, self.size, self.order = axis, size, order
        self.levels = len(order) - 1
        self.chunks = 1 << self.levels

    def key(self):
        index = lax.axis_index(self.axis)
        key = 0
        for level in range(self.levels):
            bit = lax.rem(lax.div(index, 1 << self.order[level]), 2)
            key = key + bit * (1 << (self.levels - 1 - level))
        return key

    def place(self, location, key):
        out = 0
        for bit in range(self.levels):
            own = lax.rem(lax.div(key, 1 << bit), 2)
            out = out + ((1 - own) if (location >> bit) & 1 else own) * (1 << bit)
        return out

    def permute(self, value, bit):
        return lax.ppermute(value, self.axis, [(i, i ^ (1 << bit)) for i in range(self.size)])


class Sum:
    def __init__(self, plan, keep, send):
        self.plan, self.step = plan, 0
        self.current, self.halves = None, (keep, send)
        self.flying = plan.permute(send, plan.order[0]) if plan.levels else None

    def steps(self):
        return 2 * self.plan.levels + 1

    def terms(self):
        own = self.halves[0] if self.step < self.plan.levels else self.current
        return (own, self.flying) if self.step <= self.plan.levels else None

    def advance(self, total=None):
        plan, levels = self.plan, self.plan.levels
        if self.step <= levels:
            own, arrived = self.terms()
            self.current = own + arrived if total is None else total
        else:
            self.current = jnp.concatenate([self.current, self.flying], axis=0)
        nxt = self.step + 1
        if nxt < levels:
            half = self.current.shape[0] // 2
            self.halves = (self.current[:half], self.current[half:])
            self.flying = plan.permute(self.halves[1], plan.order[nxt])
        else:
            self.flying = plan.permute(self.current, plan.order[2 * levels - nxt if nxt > levels else levels])
        self.step = nxt


    def wait_for(self, after):
        self.flying, _ = lax.optimization_barrier((self.flying, after))

    def result(self):
        return self.current, self.flying


def add_kernel(*refs):
    count = len(refs) // 3
    for n in range(count):
        refs[2 * count + n][...] = refs[2 * n][...] + refs[2 * n + 1][...]


def add_all(pairs):
    vmem = pl.BlockSpec(memory_space=pltpu.VMEM)
    return pl.pallas_call(
        add_kernel,
        out_shape=[pltpu.VMEM(own.shape, F32) for own, _ in pairs],
        in_specs=[vmem] * (2 * len(pairs)),
        out_specs=[vmem] * len(pairs),
        compiler_params=pltpu.CompilerParams(vmem_limit_bytes=LIMIT * MIB),
        cost_estimate=pl.CostEstimate(flops=ADD_FLOPS, bytes_accessed=MIB, transcendentals=0),
        name="sums",
    )(*[x for pair in pairs for x in pair])


def step_all(group, before):
    for one in group:
        one.wait_for(before)
    pairs = [one.terms() for one in group]
    totals = [None] * len(group) if None in pairs else add_all(pairs)
    for one, total in zip(group, totals):
        one.advance(total)
    return [one.current for one in group]


def run_sums(waves, feat, last, early):
    rounds = waves[0][0].steps() - 1
    levels, turns = feat.plan.levels, rounds * len(waves)
    before = last
    for turn in range(turns):
        before = step_all(waves[turn % len(waves)], before)
        if early:
            goal = 2 + (levels - 1) * turn // (turns - 2)
        else:
            goal = -(-levels * (turn + 1) // (turns - 1))
        while feat.step < min(goal, levels + 1):
            before = step_all([feat], before)
    return [one.result() for wave in waves for one in wave]


def finish(feat, after):
    while feat.step < feat.steps() - 1:
        feat.wait_for(after)
        feat.advance()
    return feat.result()


class Sizes:
    def __init__(self, mesh_shape, data_shape, cols):
        self.n_samp, self.n_feat = mesh_shape["samp"], mesh_shape["feat"]
        self.rows, self.feats = data_shape
        self.cols = cols
        bits = (self.n_samp - 1).bit_length()
        order = list(range(bits))
        self.colors = [
            Plan("samp", self.n_samp, order[n % bits:] + order[: n % bits]) for n in range(2 * HALVES)
        ]
        self.feat_plan = Plan("feat", self.n_feat, list(range((self.n_feat - 1).bit_length())))
        self.color_rows = self.feats // len(self.colors)
        self.half_rows = self.feats // HALVES
        self.coef_chunk = self.color_rows // self.colors[0].chunks
        self.share_chunk = self.rows // self.feat_plan.chunks
        self.own = self.rows // self.n_feat
        self.row_block = min(256, self.rows)
        self.feat_block = min(256, self.feats)


def coef_places(sz, half):
    out = []
    for color in range(2):
        plan = sz.colors[2 * half + color]
        key = plan.key()
        for location in range(plan.chunks):
            offset = color * sz.color_rows + plan.place(location, key) * sz.coef_chunk
            out.append((color, location, pl.multiple_of(offset, 8)))
    return out


def share_places(sz):
    key = sz.feat_plan.key()
    return [
        (location, pl.multiple_of(sz.feat_plan.place(location, key) * sz.share_chunk, 8))
        for location in range(sz.feat_plan.chunks)
    ]


def half_of(location, chunks, chunk_rows):
    half = chunks // 2
    return location // half, (location % half) * chunk_rows


def put_split(target, rows, cols, value):
    high, low = split(value)
    target[rows, :cols] = high
    target[rows, cols:] = low


def put_wide(wide_t, cols, value):
    high, low = split(value.T)
    wide_t[:cols, :] = high
    wide_t[cols:, :] = low


def triple(a_hi, a_lo, rows, value2, cols):
    wide = dot_nn(a_hi[rows, :], value2[...])
    return wide[:, :cols] + wide[:, cols:] + dot_nn(a_lo[rows, :], value2[:, :cols])


def chebyshev_steps(sz, g_hi, g_lo, resid, search, search2, total, part):
    theta, pairs = chebyshev_coefs()
    cols, block = sz.cols, sz.row_block
    blocks = [pl.ds(r * block, block) for r in range(sz.rows // block)]
    for rows in blocks:
        first = resid[rows, :] * (1.0 / theta)
        search[rows, :] = first
        total[rows, :] = first
        put_split(search2.at[0], rows, cols, first)
    for step in range(CHEB):
        last = step + 1 == CHEB
        now, later = search2.at[step % 2], search2.at[(step + 1) % 2]
        for rows in blocks:
            if step < FULL_STEPS:
                prod = triple(g_hi, g_lo, rows, now, cols)
            else:
                wide = dot_nn(g_hi[rows, :], now[...])
                prod = wide[:, :cols] + wide[:, cols:]
            if step == 0:
                part[rows, :] = prod
            else:
                part[rows, :] += prod
            if not last:
                c_old, c_res = pairs[step]
                old = search[rows, :]
                res = resid[rows, :] - old - prod
                new = c_old * old + c_res * res
                resid[rows, :] = res
                search[rows, :] = new
                total[rows, :] += new
                put_split(later, rows, cols, new)


def spread_kernel(half, sz, wide_t, a_hi, a_lo, start, dual, keep0, keep1, send0, send1, plus, proj):
    cols, block = sz.cols, min(sz.feat_block, sz.half_rows)
    base = half * sz.half_rows
    for f in range(sz.half_rows // block):
        columns = pl.ds(base + f * block, block)
        rows = pl.ds(f * block, block)
        wide = dot_nn(wide_t[...], a_hi[:, columns])
        out = wide[:cols] + wide[cols:] + dot_nn(wide_t[:cols, :], a_lo[:, columns])
        source = columns if start.shape[0] == sz.feats else rows
        value = start[source, :] + out.T
        proj[rows, :] = value
        plus[rows, :] = dual[source, :] + value
    for color, location, offset in coef_places(sz, half):
        which, row = half_of(location, sz.colors[0].chunks, sz.coef_chunk)
        target = ((keep0, keep1), (send0, send1))[which][color]
        target[pl.ds(row, sz.coef_chunk), :] = proj[pl.ds(offset, sz.coef_chunk), :]


def emit_share(sz, scratch, half_share, keep, send):
    own = pl.ds(pl.multiple_of(lax.axis_index("feat") * sz.own, 8), sz.own)
    scratch[own, :] = scratch[own, :] - half_share
    for location, offset in share_places(sz):
        which, row = half_of(location, sz.feat_plan.chunks, sz.share_chunk)
        target = (keep, send)[which]
        target[pl.ds(row, sz.share_chunk), :] = scratch[pl.ds(offset, sz.share_chunk), :]


def first_kernel(sz, data, coef_in, tile_dual_in, share_dual_in, tile_share_in, share_in, targets_in,
                 a_hi, a_lo, g_hi, g_lo, start, wide_t, keep_s, send_s, out_sum,
                 a32, coef, tile_dual, share_dual, tile_share, share, targets,
                 start2, resid, search, search2, total, part, a_sem, in_sem):
    cols, block = sz.cols, sz.row_block
    blocks = sz.rows // block
    loads = []
    for r in range(blocks):
        rows = pl.ds(r * block, block)
        loads.append(pltpu.make_async_copy(data.at[rows, :], a32.at[rows, :], a_sem.at[r]))
    smalls = [
        pltpu.make_async_copy(src, dst, in_sem.at[n]) for n, (src, dst) in enumerate((
            (coef_in, coef), (tile_dual_in, tile_dual), (share_dual_in, share_dual),
            (tile_share_in, tile_share), (share_in, share), (targets_in, targets)))
    ]
    for copy in loads + smalls:
        copy.start()
    for r in range(blocks):
        rows = pl.ds(r * block, block)
        loads[r].wait()
        high, low = split(a32[rows, :])
        a_hi[rows, :] = high
        a_lo[rows, :] = low
        for c in range(r + 1):
            others = pl.ds(c * block, block)
            gram = dot_nt(a_hi[rows, :], a_hi[others, :])
            cross = dot_nt(a_hi[rows, :], a_lo[others, :])
            if c == r:
                gram = 0.5 * gram + cross
                gram = gram + gram.T
            else:
                gram = gram + cross + dot_nt(a_lo[rows, :], a_hi[others, :])
            high, low = split(gram)
            g_hi[rows, others] = high
            g_lo[rows, others] = low
            if c != r:
                high, low = split(gram.T)
                g_hi[others, rows] = high
                g_lo[others, rows] = low
    for copy in smalls:
        copy.wait()
    first = coef[...] - tile_dual[...]
    start[...] = first
    put_split(start2, slice(None), cols, first)
    for r in range(blocks):
        rows = pl.ds(r * block, block)
        prod = triple(a_hi, a_lo, rows, start2, cols)
        out_sum[rows, :] = prod
        resid[rows, :] = tile_share[rows, :] + share_dual[rows, :] - prod
    chebyshev_steps(sz, g_hi, g_lo, resid, search, search2, total, part)
    put_wide(wide_t, cols, total[...])
    part[...] += out_sum[...]
    out_sum[...] = part[...] + share_dual[...]
    own = pl.ds(pl.multiple_of(lax.axis_index("feat") * sz.own, 8), sz.own)
    half_share = prox_share(share[...], share_dual[own, :], targets[...])
    emit_share(sz, part, half_share, keep_s, send_s)


def update_kernel(half, sz, *refs):
    before = refs[9:10] if half else ()
    a_hi, a_lo, sum00, sum01, sum10, sum11, coef, coef_dual, dual_plus = refs[:9]
    start, tile_now, half_out, coef_plus, prod, start2 = refs[9 + len(before):]
    cols, block = sz.cols, sz.row_block
    base = half * sz.half_rows
    sums = ((sum00, sum01), (sum10, sum11))
    for color, location, offset in coef_places(sz, half):
        rows = pl.ds(offset, sz.coef_chunk)
        whole = pl.ds(base + offset, sz.coef_chunk)
        which, row = half_of(location, sz.colors[0].chunks, sz.coef_chunk)
        total_coef = sums[color][which][pl.ds(row, sz.coef_chunk), :]
        dual = coef_dual[whole, :]
        prox = prox_coef(coef[whole, :] - dual)
        new = (prox + total_coef) / (sz.n_samp + 1)
        dual = dual + prox - new
        prox = prox_coef(new - dual)
        half_out[rows, :] = prox
        coef_plus[rows, :] = dual + prox
        tile = dual_plus[rows, :] - new
        tile_now[rows, :] = tile
        start[rows, :] = new - tile
    put_split(start2, slice(None), cols, start[...])
    columns = pl.ds(base, sz.half_rows)
    for r in range(sz.rows // block):
        rows = pl.ds(r * block, block)
        wide = dot_nn(a_hi[rows, columns], start2[...])
        value = wide[:, :cols] + wide[:, cols:] + dot_nn(a_lo[rows, columns], start2[:, :cols])
        prod[rows, :] = value + before[0][rows, :] if half else value


def second_kernel(sz, g_hi, g_lo, prod, esum0, esum1, out_sum, targets, share, share_dual,
                  wide_t, keep_s, send_s, half_share_out, share_dual_out, proj_share,
                  resid, search, search2, total, part):
    esums = (esum0, esum1)
    for location, offset in share_places(sz):
        rows = pl.ds(offset, sz.share_chunk)
        which, row = half_of(location, sz.feat_plan.chunks, sz.share_chunk)
        excess = esums[which][pl.ds(row, sz.share_chunk), :] * (-1.0 / (sz.n_feat + 1))
        search[rows, :] = excess
        share_dual_out[rows, :] = share_dual[rows, :] + excess
        resid[rows, :] = out_sum[rows, :] + 2.0 * excess - prod[rows, :]
    own = pl.ds(pl.multiple_of(lax.axis_index("feat") * sz.own, 8), sz.own)
    share_now = prox_share(share[...], share_dual[own, :], targets[...]) - search[own, :]
    half_share = prox_share(share_now, share_dual_out[own, :], targets[...])
    half_share_out[...] = half_share
    chebyshev_steps(sz, g_hi, g_lo, resid, search, search2, total, part)
    put_wide(wide_t, sz.cols, total[...])
    part[...] += prod[...]
    proj_share[...] = part[...]
    emit_share(sz, part, half_share, keep_s, send_s)


def last_kernel(half, sz, *refs):
    sum00, sum01, sum10, sum11, half_coef, coef_plus, tile_plus = refs[-14:-7] if not half else refs[3:10]
    outs, (new_s, dual_s, tile_s), sems = refs[-7:-4], refs[-4:-1], refs[-1]
    sums = ((sum00, sum01), (sum10, sum11))
    for color, location, offset in coef_places(sz, half):
        rows = pl.ds(offset, sz.coef_chunk)
        which, row = half_of(location, sz.colors[0].chunks, sz.coef_chunk)
        total_coef = sums[color][which][pl.ds(row, sz.coef_chunk), :]
        new = (half_coef[rows, :] + total_coef) / (sz.n_samp + 1)
        new_s[rows, :] = new
        dual_s[rows, :] = coef_plus[rows, :] - new
        tile_s[rows, :] = tile_plus[rows, :] - new
    whole = pl.ds(half * sz.half_rows, sz.half_rows)
    copies = [
        pltpu.make_async_copy(src, out.at[whole, :], sems.at[n])
        for n, (src, out) in enumerate(zip((new_s, dual_s, tile_s), outs))
    ]
    for copy in copies:
        copy.start()
    for copy in copies:
        copy.wait()


def last_share_kernel(sz, *refs):
    share_out, share_dual_out, tile_share_out = refs[-3:]
    *esums, half_share, share_dual, proj_share = refs[:-3]
    for location, offset in share_places(sz):
        rows = pl.ds(offset, sz.share_chunk)
        which, row = half_of(location, sz.feat_plan.chunks, sz.share_chunk)
        excess = esums[which][pl.ds(row, sz.share_chunk), :] * (-1.0 / (sz.n_feat + 1))
        share_dual_out[rows, :] = share_dual[rows, :] + excess
        tile_share_out[rows, :] = proj_share[rows, :] + excess
    own = pl.ds(pl.multiple_of(lax.axis_index("feat") * sz.own, 8), sz.own)
    share_out[...] = half_share[...] - (share_dual_out[own, :] - share_dual[own, :])


def shards(mesh_shape, data, targets, coef, coef_dual, tile_coef_dual, share, share_dual, tile_share):
    cols = coef.shape[1]
    sz = Sizes(mesh_shape, data.shape, cols)
    rows, feats = data.shape
    blocks = rows // sz.row_block
    f32 = lambda *shape: jax.ShapeDtypeStruct(shape, F32)
    v32 = lambda *shape: pltpu.VMEM(shape, F32)
    v16 = lambda *shape: pltpu.VMEM(shape, BF16)
    flops = 2 * rows * feats * cols

    def kernel(body, name, outs, scratch, work, limit, *operands, streamed=0, stored=False):
        vmem = pl.BlockSpec(memory_space=pltpu.VMEM)
        hbm = pl.BlockSpec(memory_space=pltpu.HBM)
        operands = [
            pltpu.with_memory_space_constraint(x, pltpu.HBM) if n < streamed else x
            for n, x in enumerate(operands)
        ]
        return pl.pallas_call(
            body,
            out_shape=outs,
            in_specs=[hbm] * streamed + [vmem] * (len(operands) - streamed),
            out_specs=[hbm if stored else vmem] * len(outs),
            scratch_shapes=scratch,
            input_output_aliases={n: n for n in range(streamed)} if stored else {},
            compiler_params=pltpu.CompilerParams(vmem_limit_bytes=limit * MIB),
            cost_estimate=pl.CostEstimate(flops=work, bytes_accessed=8 * MIB, transcendentals=0),
            name=name,
        )(*operands)

    coef_sends = [v32(sz.color_rows // 2, cols)] * 4
    share_sends = [v32(rows // 2, cols)] * 2
    matrices = [v16(rows, feats)] * 2 + [v16(rows, rows)] * 2
    vector = v32(rows, cols)
    half_coefs = v32(sz.half_rows, cols)
    wide_t = v16(2 * cols, rows)
    work = [vector, vector, v16(2, rows, 2 * cols), vector, vector]
    tile_dual = tile_coef_dual[0]

    def project(wide, keep_s, send_s, starts, duals, early):
        feat = Sum(sz.feat_plan, keep_s, send_s)
        waves, pluses = [], []
        for half in range(HALVES):
            if half:
                wide, _ = lax.optimization_barrier((wide, step_all([feat], pluses[-1]) if early else pluses[-1]))
            keep0, keep1, send0, send1, plus = kernel(
                functools.partial(spread_kernel, half, sz), f"spread{half}", coef_sends + [half_coefs],
                [half_coefs], 3 * flops // HALVES, LIMIT, wide, a_hi, a_lo, starts[half], duals[half])
            pluses.append(plus)
            waves.append([
                Sum(sz.colors[2 * half], keep0, send0), Sum(sz.colors[2 * half + 1], keep1, send1)])
        sums = run_sums(waves, feat, pluses[-1], early)
        groups = [sums[2 * half] + sums[2 * half + 1] for half in range(HALVES)]
        return groups, feat, pluses

    a_hi, a_lo, g_hi, g_lo, start, wide, keep_s, send_s, out_sum = kernel(
        functools.partial(first_kernel, sz), "first",
        matrices + [v32(feats, cols), wide_t] + share_sends + [vector],
        [v32(rows, feats), v32(feats, cols), v32(feats, cols), vector, vector, v32(sz.own, cols),
         v32(sz.own, cols), v16(feats, 2 * cols)] + work
        + [pltpu.SemaphoreType.DMA((blocks,)), pltpu.SemaphoreType.DMA((6,))], 30 * flops, 24,
        data, coef, tile_dual, share_dual, tile_share[0], share, targets, streamed=7)
    groups, feat, pluses = project(wide, keep_s, send_s, [start] * HALVES, [tile_dual] * HALVES, True)
    esums = finish(feat, groups[0][0])
    starts, duals, saved, prod = [], [], [], []
    for half in range(HALVES):
        start, tile_now, half_coef, coef_plus, total = kernel(
            functools.partial(update_kernel, half, sz), f"update{half}", [half_coefs] * 4 + [vector],
            [v16(sz.half_rows, 2 * cols)], 2 * ADD_FLOPS, LIMIT,
            a_hi, a_lo, *groups[half], coef, coef_dual, pluses[half], *prod)
        starts.append(start)
        duals.append(tile_now)
        saved.append((half_coef, coef_plus))
        prod = [total]
    wide, keep_s, send_s, half_share, dual_now, proj_share = kernel(
        functools.partial(second_kernel, sz), "second",
        [wide_t] + share_sends + [v32(sz.own, cols), vector, vector],
        work, 11 * flops, LIMIT, g_hi, g_lo, *prod, *esums, out_sum, targets, share, share_dual)
    groups, feat, pluses = project(wide, keep_s, send_s, starts, duals, False)
    finals = []
    for half in range(HALVES):
        finals = kernel(
            functools.partial(last_kernel, half, sz), f"last{half}", [f32(feats, cols)] * 3,
            [half_coefs] * 3 + [pltpu.SemaphoreType.DMA((3,))], 2 * ADD_FLOPS, LIMIT,
            *finals, *groups[half], *saved[half], pluses[half], streamed=len(finals), stored=True)
    coef_out, coef_dual_out, tile_out = finals
    esums = finish(feat, coef_out)
    share_out, share_dual_out, tile_share_out = kernel(
        functools.partial(last_share_kernel, sz), "last_share",
        [f32(sz.own, cols), f32(rows, cols), f32(rows, cols)],
        [], flops // 100, LIMIT, *esums, half_share, dual_now, proj_share)
    return (coef_out, coef_dual_out, tile_out[None], share_out, share_dual_out, tile_share_out[None])


def solution(mesh):
    mesh_shape = dict(mesh.shape)
    return jax.shard_map(
        functools.partial(shards, mesh_shape),
        mesh=mesh,
        in_specs=(
            P("samp", "feat"),
            P(("samp", "feat"), None),
            P("feat", None),
            P("feat", None),
            P("samp", "feat", None),
            P(("samp", "feat"), None),
            P("samp", None),
            P("feat", "samp", None),
        ),
        out_specs=(
            P("feat", None),
            P("feat", None),
            P("samp", "feat", None),
            P(("samp", "feat"), None),
            P("samp", None),
            P("feat", "samp", None),
        ),
        check_vma=False,
    )
```

```python
import functools

import jax
import jax.numpy as jnp
from jax import lax
from jax.experimental import pallas as pl
from jax.experimental.pallas import tpu as pltpu
from jax.sharding import PartitionSpec as P

CHEB = 5

cheb_low = 1.0
cheb_high = 3.2
l1_weight = 0.2
huber_width = 4.0

F32 = jnp.float32
BF16 = jnp.bfloat16
MIB = 1 << 20
LIMIT = 16
HALVES = 2
FULL_STEPS = 4
ADD_FLOPS = 4 * 10**9


def chebyshev_coefs():
    theta = (cheb_high + cheb_low) / 2.0
    delta = (cheb_high - cheb_low) / 2.0
    sigma = theta / delta
    rho = 1.0 / sigma
    pairs = []
    for _ in range(CHEB - 1):
        rho_new = 1.0 / (2.0 * sigma - rho)
        pairs.append((rho_new * rho, 2.0 * rho_new / delta))
        rho = rho_new
    return theta, pairs


def split(value):
    high = value.astype(BF16)
    return high, (value - high.astype(F32)).astype(BF16)


def dot_nn(a, b):
    return jnp.dot(a, b, preferred_element_type=F32)


def dot_nt(a, b):
    return lax.dot_general(a, b, (((1,), (1,)), ((), ())), preferred_element_type=F32)


def prox_coef(value):
    return value - jnp.clip(value, -l1_weight, l1_weight)


def prox_share(share, dual, targets):
    resid = share - dual - targets
    return targets + resid - jnp.clip(resid / 2.0, -huber_width, huber_width)


class Plan:
    def __init__(self, axis, size, order):
        self.axis, self.size, self.order = axis, size, order
        self.levels = len(order) - 1
        self.chunks = 1 << self.levels

    def key(self):
        index = lax.axis_index(self.axis)
        key = 0
        for level in range(self.levels):
            bit = lax.rem(lax.div(index, 1 << self.order[level]), 2)
            key = key + bit * (1 << (self.levels - 1 - level))
        return key

    def place(self, location, key):
        out = 0
        for bit in range(self.levels):
            own = lax.rem(lax.div(key, 1 << bit), 2)
            out = out + ((1 - own) if (location >> bit) & 1 else own) * (1 << bit)
        return out

    def permute(self, value, bit):
        return lax.ppermute(value, self.axis, [(i, i ^ (1 << bit)) for i in range(self.size)])


class Sum:
    def __init__(self, plan, keep, send):
        self.plan, self.step = plan, 0
        self.current, self.halves = None, (keep, send)
        self.flying = plan.permute(send, plan.order[0]) if plan.levels else None

    def steps(self):
        return 2 * self.plan.levels + 1

    def terms(self):
        own = self.halves[0] if self.step < self.plan.levels else self.current
        return (own, self.flying) if self.step <= self.plan.levels else None

    def advance(self, total=None):
        plan, levels = self.plan, self.plan.levels
        if self.step <= levels:
            own, arrived = self.terms()
            self.current = own + arrived if total is None else total
        else:
            self.current = jnp.concatenate([self.current, self.flying], axis=0)
        nxt = self.step + 1
        if nxt < levels:
            half = self.current.shape[0] // 2
            self.halves = (self.current[:half], self.current[half:])
            self.flying = plan.permute(self.halves[1], plan.order[nxt])
        else:
            self.flying = plan.permute(self.current, plan.order[2 * levels - nxt if nxt > levels else levels])
        self.step = nxt


    def wait_for(self, after):
        self.flying, _ = lax.optimization_barrier((self.flying, after))

    def result(self):
        return self.current, self.flying


def add_kernel(*refs):
    count = len(refs) // 3
    for n in range(count):
        refs[2 * count + n][...] = refs[2 * n][...] + refs[2 * n + 1][...]


def add_all(pairs):
    vmem = pl.BlockSpec(memory_space=pltpu.VMEM)
    return pl.pallas_call(
        add_kernel,
        out_shape=[pltpu.VMEM(own.shape, F32) for own, _ in pairs],
        in_specs=[vmem] * (2 * len(pairs)),
        out_specs=[vmem] * len(pairs),
        compiler_params=pltpu.CompilerParams(vmem_limit_bytes=LIMIT * MIB),
        cost_estimate=pl.CostEstimate(flops=ADD_FLOPS, bytes_accessed=MIB, transcendentals=0),
        name="sums",
    )(*[x for pair in pairs for x in pair])


def step_all(group, before):
    for one in group:
        one.wait_for(before)
    pairs = [one.terms() for one in group]
    totals = [None] * len(group) if None in pairs else add_all(pairs)
    for one, total in zip(group, totals):
        one.advance(total)
    return [one.current for one in group]


def run_sums(waves, feat, last, early):
    rounds = waves[0][0].steps() - 1
    levels, turns = feat.plan.levels, rounds * len(waves)
    before = last
    for turn in range(turns):
        before = step_all(waves[turn % len(waves)], before)
        if early:
            goal = 2 + (levels - 1) * turn // (turns - 2)
        else:
            goal = -(-levels * (turn + 1) // (turns - 1))
        while feat.step < min(goal, levels + 1):
            before = step_all([feat], before)
    return [one.result() for wave in waves for one in wave]


def finish(feat, after):
    while feat.step < feat.steps() - 1:
        feat.wait_for(after)
        feat.advance()
    return feat.result()


class Sizes:
    def __init__(self, mesh_shape, data_shape, cols):
        self.n_samp, self.n_feat = mesh_shape["samp"], mesh_shape["feat"]
        self.rows, self.feats = data_shape
        self.cols = cols
        bits = (self.n_samp - 1).bit_length()
        order = list(range(bits))
        self.colors = [
            Plan("samp", self.n_samp, order[n % bits:] + order[: n % bits]) for n in range(2 * HALVES)
        ]
        self.feat_plan = Plan("feat", self.n_feat, list(range((self.n_feat - 1).bit_length())))
        self.color_rows = self.feats // len(self.colors)
        self.half_rows = self.feats // HALVES
        self.coef_chunk = self.color_rows // self.colors[0].chunks
        self.share_chunk = self.rows // self.feat_plan.chunks
        self.own = self.rows // self.n_feat
        self.row_block = min(256, self.rows)
        self.feat_block = min(256, self.feats)


def coef_places(sz, half):
    out = []
    for color in range(2):
        plan = sz.colors[2 * half + color]
        key = plan.key()
        for location in range(plan.chunks):
            offset = color * sz.color_rows + plan.place(location, key) * sz.coef_chunk
            out.append((color, location, pl.multiple_of(offset, 8)))
    return out


def share_places(sz):
    key = sz.feat_plan.key()
    return [
        (location, pl.multiple_of(sz.feat_plan.place(location, key) * sz.share_chunk, 8))
        for location in range(sz.feat_plan.chunks)
    ]


def half_of(location, chunks, chunk_rows):
    half = chunks // 2
    return location // half, (location % half) * chunk_rows


def put_split(target, rows, cols, value):
    high, low = split(value)
    target[rows, :cols] = high
    target[rows, cols:] = low


def put_wide(wide_t, cols, value):
    high, low = split(value.T)
    wide_t[:cols, :] = high
    wide_t[cols:, :] = low


def triple(a_hi, a_lo, rows, value2, cols):
    wide = dot_nn(a_hi[rows, :], value2[...])
    return wide[:, :cols] + wide[:, cols:] + dot_nn(a_lo[rows, :], value2[:, :cols])


def chebyshev_steps(sz, g_hi, g_lo, resid, search, search2, total, part):
    theta, pairs = chebyshev_coefs()
    cols, block = sz.cols, sz.row_block
    blocks = [pl.ds(r * block, block) for r in range(sz.rows // block)]
    for rows in blocks:
        part[rows, :] = resid[rows, :]
        first = resid[rows, :] * (1.0 / theta)
        search[rows, :] = first
        total[rows, :] = first
        put_split(search2.at[0], rows, cols, first)
    for step in range(CHEB):
        last = step + 1 == CHEB
        now, later = search2.at[step % 2], search2.at[(step + 1) % 2]
        for rows in blocks:
            if step < FULL_STEPS:
                prod = triple(g_hi, g_lo, rows, now, cols)
            else:
                wide = dot_nn(g_hi[rows, :], now[...])
                prod = wide[:, :cols] + wide[:, cols:]
            if last:
                settled = resid[rows, :] + (total[rows, :] - search[rows, :])
                part[rows, :] = (part[rows, :] - settled) + prod
            else:
                c_old, c_res = pairs[step]
                old = search[rows, :]
                res = resid[rows, :] - old - prod
                new = c_old * old + c_res * res
                resid[rows, :] = res
                search[rows, :] = new
                total[rows, :] += new
                put_split(later, rows, cols, new)


def spread_kernel(half, sz, wide_t, a_hi, a_lo, start, dual, keep0, keep1, send0, send1, plus, proj):
    cols, block = sz.cols, min(sz.feat_block, sz.half_rows)
    base = half * sz.half_rows
    for f in range(sz.half_rows // block):
        columns = pl.ds(base + f * block, block)
        rows = pl.ds(f * block, block)
        wide = dot_nn(wide_t[...], a_hi[:, columns])
        out = wide[:cols] + wide[cols:] + dot_nn(wide_t[:cols, :], a_lo[:, columns])
        source = columns if start.shape[0] == sz.feats else rows
        value = start[source, :] + out.T
        proj[rows, :] = value
        plus[rows, :] = dual[source, :] + value
    for color, location, offset in coef_places(sz, half):
        which, row = half_of(location, sz.colors[0].chunks, sz.coef_chunk)
        target = ((keep0, keep1), (send0, send1))[which][color]
        target[pl.ds(row, sz.coef_chunk), :] = proj[pl.ds(offset, sz.coef_chunk), :]


def emit_share(sz, scratch, half_share, keep, send):
    own = pl.ds(pl.multiple_of(lax.axis_index("feat") * sz.own, 8), sz.own)
    scratch[own, :] = scratch[own, :] - half_share
    for location, offset in share_places(sz):
        which, row = half_of(location, sz.feat_plan.chunks, sz.share_chunk)
        target = (keep, send)[which]
        target[pl.ds(row, sz.share_chunk), :] = scratch[pl.ds(offset, sz.share_chunk), :]


def first_kernel(sz, data, coef_in, tile_dual_in, share_dual_in, tile_share_in, share_in, targets_in,
                 a_hi, a_lo, g_hi, g_lo, start, wide_t, keep_s, send_s, out_sum,
                 a32, coef, tile_dual, share_dual, tile_share, share, targets,
                 start2, resid, search, search2, total, part, a_sem, in_sem):
    cols, block = sz.cols, sz.row_block
    blocks = sz.rows // block
    loads = []
    for r in range(blocks):
        rows = pl.ds(r * block, block)
        loads.append(pltpu.make_async_copy(data.at[rows, :], a32.at[rows, :], a_sem.at[r]))
    smalls = [
        pltpu.make_async_copy(src, dst, in_sem.at[n]) for n, (src, dst) in enumerate((
            (coef_in, coef), (tile_dual_in, tile_dual), (share_dual_in, share_dual),
            (tile_share_in, tile_share), (share_in, share), (targets_in, targets)))
    ]
    for copy in loads + smalls:
        copy.start()
    for r in range(blocks):
        rows = pl.ds(r * block, block)
        loads[r].wait()
        high, low = split(a32[rows, :])
        a_hi[rows, :] = high
        a_lo[rows, :] = low
        for c in range(r + 1):
            others = pl.ds(c * block, block)
            gram = dot_nt(a_hi[rows, :], a_hi[others, :])
            cross = dot_nt(a_hi[rows, :], a_lo[others, :])
            if c == r:
                gram = 0.5 * gram + cross
                gram = gram + gram.T
            else:
                gram = gram + cross + dot_nt(a_lo[rows, :], a_hi[others, :])
            high, low = split(gram)
            g_hi[rows, others] = high
            g_lo[rows, others] = low
            if c != r:
                high, low = split(gram.T)
                g_hi[others, rows] = high
                g_lo[others, rows] = low
    for copy in smalls:
        copy.wait()
    first = coef[...] - tile_dual[...]
    start[...] = first
    put_split(start2, slice(None), cols, first)
    for r in range(blocks):
        rows = pl.ds(r * block, block)
        prod = triple(a_hi, a_lo, rows, start2, cols)
        out_sum[rows, :] = prod
        resid[rows, :] = tile_share[rows, :] + share_dual[rows, :] - prod
    chebyshev_steps(sz, g_hi, g_lo, resid, search, search2, total, part)
    put_wide(wide_t, cols, total[...])
    part[...] += out_sum[...]
    out_sum[...] = part[...] + share_dual[...]
    own = pl.ds(pl.multiple_of(lax.axis_index("feat") * sz.own, 8), sz.own)
    half_share = prox_share(share[...], share_dual[own, :], targets[...])
    emit_share(sz, part, half_share, keep_s, send_s)


def update_kernel(half, sz, *refs):
    before = refs[9:10] if half else ()
    a_hi, a_lo, sum00, sum01, sum10, sum11, coef, coef_dual, dual_plus = refs[:9]
    start, tile_now, half_out, coef_plus, prod, start2 = refs[9 + len(before):]
    cols, block = sz.cols, sz.row_block
    base = half * sz.half_rows
    sums = ((sum00, sum01), (sum10, sum11))
    for color, location, offset in coef_places(sz, half):
        rows = pl.ds(offset, sz.coef_chunk)
        whole = pl.ds(base + offset, sz.coef_chunk)
        which, row = half_of(location, sz.colors[0].chunks, sz.coef_chunk)
        total_coef = sums[color][which][pl.ds(row, sz.coef_chunk), :]
        dual = coef_dual[whole, :]
        prox = prox_coef(coef[whole, :] - dual)
        new = (prox + total_coef) / (sz.n_samp + 1)
        dual = dual + prox - new
        prox = prox_coef(new - dual)
        half_out[rows, :] = prox
        coef_plus[rows, :] = dual + prox
        tile = dual_plus[rows, :] - new
        tile_now[rows, :] = tile
        start[rows, :] = new - tile
    put_split(start2, slice(None), cols, start[...])
    columns = pl.ds(base, sz.half_rows)
    for r in range(sz.rows // block):
        rows = pl.ds(r * block, block)
        wide = dot_nn(a_hi[rows, columns], start2[...])
        value = wide[:, :cols] + wide[:, cols:] + dot_nn(a_lo[rows, columns], start2[:, :cols])
        prod[rows, :] = value + before[0][rows, :] if half else value


def second_kernel(sz, g_hi, g_lo, prod, esum0, esum1, out_sum, targets, share, share_dual,
                  wide_t, keep_s, send_s, half_share_out, share_dual_out, proj_share,
                  resid, search, search2, total, part):
    esums = (esum0, esum1)
    for location, offset in share_places(sz):
        rows = pl.ds(offset, sz.share_chunk)
        which, row = half_of(location, sz.feat_plan.chunks, sz.share_chunk)
        excess = esums[which][pl.ds(row, sz.share_chunk), :] * (-1.0 / (sz.n_feat + 1))
        search[rows, :] = excess
        share_dual_out[rows, :] = share_dual[rows, :] + excess
        resid[rows, :] = out_sum[rows, :] + 2.0 * excess - prod[rows, :]
    own = pl.ds(pl.multiple_of(lax.axis_index("feat") * sz.own, 8), sz.own)
    share_now = prox_share(share[...], share_dual[own, :], targets[...]) - search[own, :]
    half_share = prox_share(share_now, share_dual_out[own, :], targets[...])
    half_share_out[...] = half_share
    chebyshev_steps(sz, g_hi, g_lo, resid, search, search2, total, part)
    put_wide(wide_t, sz.cols, total[...])
    part[...] += prod[...]
    proj_share[...] = part[...]
    emit_share(sz, part, half_share, keep_s, send_s)


def last_kernel(half, sz, *refs):
    sum00, sum01, sum10, sum11, half_coef, coef_plus, tile_plus = refs[-14:-7] if not half else refs[3:10]
    outs, (new_s, dual_s, tile_s), sems = refs[-7:-4], refs[-4:-1], refs[-1]
    sums = ((sum00, sum01), (sum10, sum11))
    for color, location, offset in coef_places(sz, half):
        rows = pl.ds(offset, sz.coef_chunk)
        which, row = half_of(location, sz.colors[0].chunks, sz.coef_chunk)
        total_coef = sums[color][which][pl.ds(row, sz.coef_chunk), :]
        new = (half_coef[rows, :] + total_coef) / (sz.n_samp + 1)
        new_s[rows, :] = new
        dual_s[rows, :] = coef_plus[rows, :] - new
        tile_s[rows, :] = tile_plus[rows, :] - new
    whole = pl.ds(half * sz.half_rows, sz.half_rows)
    copies = [
        pltpu.make_async_copy(src, out.at[whole, :], sems.at[n])
        for n, (src, out) in enumerate(zip((new_s, dual_s, tile_s), outs))
    ]
    for copy in copies:
        copy.start()
    for copy in copies:
        copy.wait()


def last_share_kernel(sz, *refs):
    share_out, share_dual_out, tile_share_out = refs[-3:]
    *esums, half_share, share_dual, proj_share = refs[:-3]
    for location, offset in share_places(sz):
        rows = pl.ds(offset, sz.share_chunk)
        which, row = half_of(location, sz.feat_plan.chunks, sz.share_chunk)
        excess = esums[which][pl.ds(row, sz.share_chunk), :] * (-1.0 / (sz.n_feat + 1))
        share_dual_out[rows, :] = share_dual[rows, :] + excess
        tile_share_out[rows, :] = proj_share[rows, :] + excess
    own = pl.ds(pl.multiple_of(lax.axis_index("feat") * sz.own, 8), sz.own)
    share_out[...] = half_share[...] - (share_dual_out[own, :] - share_dual[own, :])


def shards(mesh_shape, data, targets, coef, coef_dual, tile_coef_dual, share, share_dual, tile_share):
    cols = coef.shape[1]
    sz = Sizes(mesh_shape, data.shape, cols)
    rows, feats = data.shape
    blocks = rows // sz.row_block
    f32 = lambda *shape: jax.ShapeDtypeStruct(shape, F32)
    v32 = lambda *shape: pltpu.VMEM(shape, F32)
    v16 = lambda *shape: pltpu.VMEM(shape, BF16)
    flops = 2 * rows * feats * cols

    def kernel(body, name, outs, scratch, work, limit, *operands, streamed=0, stored=False):
        vmem = pl.BlockSpec(memory_space=pltpu.VMEM)
        hbm = pl.BlockSpec(memory_space=pltpu.HBM)
        operands = [
            pltpu.with_memory_space_constraint(x, pltpu.HBM) if n < streamed else x
            for n, x in enumerate(operands)
        ]
        return pl.pallas_call(
            body,
            out_shape=outs,
            in_specs=[hbm] * streamed + [vmem] * (len(operands) - streamed),
            out_specs=[hbm if stored else vmem] * len(outs),
            scratch_shapes=scratch,
            input_output_aliases={n: n for n in range(streamed)} if stored else {},
            compiler_params=pltpu.CompilerParams(vmem_limit_bytes=limit * MIB),
            cost_estimate=pl.CostEstimate(flops=work, bytes_accessed=8 * MIB, transcendentals=0),
            name=name,
        )(*operands)

    coef_sends = [v32(sz.color_rows // 2, cols)] * 4
    share_sends = [v32(rows // 2, cols)] * 2
    matrices = [v16(rows, feats)] * 2 + [v16(rows, rows)] * 2
    vector = v32(rows, cols)
    half_coefs = v32(sz.half_rows, cols)
    wide_t = v16(2 * cols, rows)
    work = [vector, vector, v16(2, rows, 2 * cols), vector, vector]
    tile_dual = tile_coef_dual[0]

    def project(wide, keep_s, send_s, starts, duals, early):
        feat = Sum(sz.feat_plan, keep_s, send_s)
        waves, pluses = [], []
        for half in range(HALVES):
            if half:
                wide, _ = lax.optimization_barrier((wide, step_all([feat], pluses[-1]) if early else pluses[-1]))
            keep0, keep1, send0, send1, plus = kernel(
                functools.partial(spread_kernel, half, sz), f"spread{half}", coef_sends + [half_coefs],
                [half_coefs], 3 * flops // HALVES, LIMIT, wide, a_hi, a_lo, starts[half], duals[half])
            pluses.append(plus)
            waves.append([
                Sum(sz.colors[2 * half], keep0, send0), Sum(sz.colors[2 * half + 1], keep1, send1)])
        sums = run_sums(waves, feat, pluses[-1], early)
        groups = [sums[2 * half] + sums[2 * half + 1] for half in range(HALVES)]
        return groups, feat, pluses

    a_hi, a_lo, g_hi, g_lo, start, wide, keep_s, send_s, out_sum = kernel(
        functools.partial(first_kernel, sz), "first",
        matrices + [v32(feats, cols), wide_t] + share_sends + [vector],
        [v32(rows, feats), v32(feats, cols), v32(feats, cols), vector, vector, v32(sz.own, cols),
         v32(sz.own, cols), v16(feats, 2 * cols)] + work
        + [pltpu.SemaphoreType.DMA((blocks,)), pltpu.SemaphoreType.DMA((6,))], 30 * flops, 24,
        data, coef, tile_dual, share_dual, tile_share[0], share, targets, streamed=7)
    groups, feat, pluses = project(wide, keep_s, send_s, [start] * HALVES, [tile_dual] * HALVES, True)
    esums = finish(feat, groups[0][0])
    starts, duals, saved, prod = [], [], [], []
    for half in range(HALVES):
        start, tile_now, half_coef, coef_plus, total = kernel(
            functools.partial(update_kernel, half, sz), f"update{half}", [half_coefs] * 4 + [vector],
            [v16(sz.half_rows, 2 * cols)], 2 * ADD_FLOPS, LIMIT,
            a_hi, a_lo, *groups[half], coef, coef_dual, pluses[half], *prod)
        starts.append(start)
        duals.append(tile_now)
        saved.append((half_coef, coef_plus))
        prod = [total]
    wide, keep_s, send_s, half_share, dual_now, proj_share = kernel(
        functools.partial(second_kernel, sz), "second",
        [wide_t] + share_sends + [v32(sz.own, cols), vector, vector],
        work, 11 * flops, LIMIT, g_hi, g_lo, *prod, *esums, out_sum, targets, share, share_dual)
    groups, feat, pluses = project(wide, keep_s, send_s, starts, duals, False)
    finals = []
    for half in range(HALVES):
        finals = kernel(
            functools.partial(last_kernel, half, sz), f"last{half}", [f32(feats, cols)] * 3,
            [half_coefs] * 3 + [pltpu.SemaphoreType.DMA((3,))], 2 * ADD_FLOPS, LIMIT,
            *finals, *groups[half], *saved[half], pluses[half], streamed=len(finals), stored=True)
        if half == 0:
            esums = finish(feat, finals[0])
    coef_out, coef_dual_out, tile_out = finals
    share_out, share_dual_out, tile_share_out = kernel(
        functools.partial(last_share_kernel, sz), "last_share",
        [f32(sz.own, cols), f32(rows, cols), f32(rows, cols)],
        [], flops // 100, LIMIT, *esums, half_share, dual_now, proj_share)
    return (coef_out, coef_dual_out, tile_out[None], share_out, share_dual_out, tile_share_out[None])


def solution(mesh):
    mesh_shape = dict(mesh.shape)
    return jax.shard_map(
        functools.partial(shards, mesh_shape),
        mesh=mesh,
        in_specs=(
            P("samp", "feat"),
            P(("samp", "feat"), None),
            P("feat", None),
            P("feat", None),
            P("samp", "feat", None),
            P(("samp", "feat"), None),
            P("samp", None),
            P("feat", "samp", None),
        ),
        out_specs=(
            P("feat", None),
            P("feat", None),
            P("samp", "feat", None),
            P(("samp", "feat"), None),
            P("samp", None),
            P("feat", "samp", None),
        ),
        check_vma=False,
    )
```
